32 devices in a mesh: dp: 4 (over x, core), mp: 8 (over z, y).
Axes of the slice: x: 2, y: 2, z: 4, core: 2. Of those that a mesh axis runs over, the one named last changes fastest.
Arguments:
- prelude_output: bfloat16 [12, 32, 5280], P('dp', None, 'mp'), may hold values from -6 to 6
- init_noise: bfloat16 [16, 32, 5280], P('dp', None, 'mp'), may hold values from -6 to 6
- core_weight: bfloat16 [5280, 5280], P('mp'), may hold values from -0.078125 to 0.078125
- norm_gain: float32 [5280], replicated, may hold values from 0.5 to 1.5
- state_cotangent: bfloat16 [16, 32, 5280], P('dp', None, 'mp'), may hold values from -6 to 6
- step_counts: int32 [12], replicated, may hold values from 1 to 3, as said below
- group_table: int32 [12], replicated, may hold values from 0 to 3, as said below
Outputs:
- weight_grad: float32 [5280, 5280], P('mp', 'dp')
The draws below stay inside these ranges and needn't reach their ends.
Inputs may be any that keep to these rules, and one draw needn't show every extreme that they name: `step_counts`: sequences in the groups that run fewer sequences all take 3 steps. `group_table`: half of the groups run 4 sequences and the other half run 2 (their other 2 slots stay empty).
All inputs are finite; a program needn't handle non-finite values.
Results may differ from the reference program's by a relative error of at most 0.025.
Values may be sent and summed in bfloat16 or wider, within the bound.
A program may use at most 64 MiB of HBM per device.

```python
import jax
import jax.numpy as jnp
from jax import lax

MODEL_WIDTH = 5280
TOKEN_LENGTH = 32
SEQ_DEV = 3
CAP = 4
MAXR = 3
BP = 2
SEQS = 12
SEQUENCE_SLOTS = 16
N_DP = 4
N_MP = 8


def deal_sequences(key):
    base_key = jax.random.fold_in(key, 11)
    order_key, group_key, count_key = jax.random.split(base_key, 3)
    group_total = SEQS // SEQ_DEV
    group_halves = group_total // 2
    light_size = CAP
    heavy_size = 2 * SEQ_DEV - CAP
    heavy_total = group_halves * heavy_size
    seq_order = jax.random.permutation(order_key, SEQS).astype(jnp.int32)
    group_order = jax.random.permutation(group_key, group_total).astype(jnp.int32)
    position = jnp.arange(SEQS, dtype=jnp.int32)
    is_heavy = position < heavy_total
    heavy_slot = jnp.clip(position // heavy_size, 0, group_total - 1)
    light_slot = jnp.clip(group_halves + (position - heavy_total) // light_size, 0, group_total - 1)
    group_at = jnp.where(is_heavy, group_order[heavy_slot], group_order[light_slot])
    light_counts = jax.random.randint(count_key, (SEQS,), 1, MAXR).astype(jnp.int32)
    count_at = jnp.where(is_heavy, MAXR, light_counts).astype(jnp.int32)
    table = jnp.zeros((SEQS,), jnp.int32).at[seq_order].set(group_at)
    counts = jnp.zeros((SEQS,), jnp.int32).at[seq_order].set(count_at)
    return (counts, table)


def draw_step_counts(key, part):
    counts, table = deal_sequences(key)
    return counts


def draw_group_table(key, part):
    counts, table = deal_sequences(key)
    return table


def steps_of(rng, shape, shards, least, high):
    def one(dim, blocks):
        steps = jax.random.uniform(jax.random.fold_in(jax.random.fold_in(rng, 6), dim), (blocks,), jnp.float32, least / len(shards), high / len(shards))
        return jnp.repeat(jnp.exp(steps), shape[dim] // blocks).reshape((-1,) + (1,) * (len(shape) - dim - 1))

    gain = one(*shards[0])
    for cut in shards[1:]:
        gain = gain * one(*cut)
    return gain


def centred(own_key, dims, scale, bound, cuts=(), held_as=jnp.bfloat16):
    loudness = steps_of(own_key, dims, cuts, -0.22, 0.18) if cuts else 1.0
    array = jax.random.normal(own_key, dims, jnp.float32) * scale * loudness
    return jnp.minimum(jnp.maximum(array, -bound), bound).astype(held_as)


def setup_inputs(seed: int = 0) -> dict:
    keys = jax.random.split(jax.random.key(seed), 8)
    return {
        "prelude_output": centred(keys[0], (SEQS, TOKEN_LENGTH, MODEL_WIDTH), 1.0, 6.0, ((0, 4), (2, 8))),
        "init_noise": centred(keys[1], (SEQUENCE_SLOTS, TOKEN_LENGTH, MODEL_WIDTH), 1.0, 6.0, ((0, 4), (2, 8))),
        "core_weight": centred(keys[2], (MODEL_WIDTH, MODEL_WIDTH), MODEL_WIDTH ** -0.5, 0.078125, ((0, 8),)),
        "norm_gain": jnp.clip(1.0 + 0.1 * jax.random.normal(keys[3], (MODEL_WIDTH,), jnp.float32), 0.5, 1.5),
        "state_cotangent": centred(keys[4], (SEQUENCE_SLOTS, TOKEN_LENGTH, MODEL_WIDTH), 1.0, 6.0, ((0, 4), (2, 8))),
        "step_counts": draw_step_counts(jax.random.fold_in(keys[7], 71), 0),
        "group_table": draw_group_table(jax.random.fold_in(keys[7], 71), 0),
    }


EPS = 1e-06

def block_sum(delta_b, core_weight):
    block_width = MODEL_WIDTH // N_MP

    def add_block(running, block_index):
        first_row = block_index * block_width
        delta_cols = lax.dynamic_slice_in_dim(delta_b, first_row, block_width, 1)
        weight_rows = lax.dynamic_slice_in_dim(core_weight, first_row, block_width, 0)
        product = jnp.dot(delta_cols, weight_rows, preferred_element_type=jnp.float32)
        rounded = lax.optimization_barrier(product.astype(jnp.bfloat16)).astype(jnp.float32)
        return (running + rounded, None)
    start_value = jnp.zeros((delta_b.shape[0], MODEL_WIDTH), jnp.float32)
    finished, unused = lax.scan(add_block, start_value, jnp.arange(N_MP, dtype=jnp.int32))
    return finished

def reference(prelude_output, init_noise, core_weight, norm_gain, state_cotangent, step_counts, group_table):
    seq_index = jnp.arange(SEQS, dtype=jnp.int32)
    earlier = (group_table[:, None] == group_table[None, :]) & (seq_index[None, :] < seq_index[:, None])
    slot_rank = lax.optimization_barrier(jnp.sum(earlier.astype(jnp.int32), axis=1))
    placed = group_table * CAP + slot_rank
    slot_index = jnp.arange(SEQUENCE_SLOTS, dtype=jnp.int32)
    selected_rows = placed[None, :] == slot_index[:, None]
    injected_input = jnp.einsum('gu,uhv->ghv', selected_rows.astype(jnp.float32), prelude_output.astype(jnp.float32), precision=lax.Precision.HIGHEST).reshape(SEQUENCE_SLOTS * TOKEN_LENGTH, MODEL_WIDTH)
    slot_counts = lax.optimization_barrier(jnp.sum(jnp.where(selected_rows, step_counts[None, :], 0), axis=1))
    state = init_noise.reshape(SEQUENCE_SLOTS * TOKEN_LENGTH, MODEL_WIDTH)
    saved = []
    for turn in range(MAXR):
        active = jnp.repeat(turn >= MAXR - slot_counts, TOKEN_LENGTH)[:, None]
        product = lax.dot_general(state, core_weight, (((1,), (1,)), ((), ())), preferred_element_type=jnp.float32)
        mixed = (product + injected_input).astype(jnp.bfloat16)
        mixed_float = mixed.astype(jnp.float32)
        inverse_rms = lax.rsqrt(lax.optimization_barrier(jnp.sum(mixed_float * mixed_float, axis=1)) / MODEL_WIDTH + EPS)
        renewed = (norm_gain * mixed_float * inverse_rms[:, None]).astype(jnp.bfloat16)
        saved.append((state, mixed_float, inverse_rms, active))
        state = jnp.where(active, renewed, state)
    upstream = state_cotangent.reshape(SEQUENCE_SLOTS * TOKEN_LENGTH, MODEL_WIDTH).astype(jnp.float32)
    delta_list = []
    state_list = []
    for back_index in range(BP):
        state_in, mixed_float, inverse_rms, active = saved[MAXR - 1 - back_index]
        scaled = upstream * norm_gain
        inner = lax.optimization_barrier(jnp.sum(scaled * mixed_float, axis=1))
        delta = inverse_rms[:, None] * scaled - mixed_float * (inverse_rms ** 3 * inner / MODEL_WIDTH)[:, None]
        delta_b = jnp.where(active, delta, 0.0).astype(jnp.bfloat16)
        delta_list.append(delta_b)
        state_list.append(state_in)
        if back_index + 1 < BP:
            upstream = jnp.where(active, block_sum(delta_b, core_weight), upstream)
    group_rows = CAP * TOKEN_LENGTH
    deltas = jnp.stack(delta_list).reshape(BP, N_DP, group_rows, MODEL_WIDTH).transpose(1, 0, 2, 3)
    states = jnp.stack(state_list).reshape(BP, N_DP, group_rows, MODEL_WIDTH).transpose(1, 0, 2, 3)

    def add_group(total, pieces):
        group_deltas, group_states = pieces
        partial_grad = jnp.zeros((MODEL_WIDTH, MODEL_WIDTH), jnp.float32)
        for back_index in range(BP):
            partial_grad = partial_grad + lax.dot_general(group_deltas[back_index], group_states[back_index], (((0,), (0,)), ((), ())), preferred_element_type=jnp.float32)
        rounded = lax.optimization_barrier(partial_grad.astype(jnp.bfloat16)).astype(jnp.float32)
        return (total + rounded, None)
    weight_grad, unused = lax.scan(add_group, jnp.zeros((MODEL_WIDTH, MODEL_WIDTH), jnp.float32), (deltas, states))
    return weight_grad
```

```python
import functools

import jax
import jax.numpy as jnp
from jax import lax
from jax.experimental import pallas as pl
from jax.experimental.pallas import tpu as pltpu
from jax.sharding import PartitionSpec as P

MESH = pl.DeviceIdType.MESH
NT = (((1,), (1,)), ((), ()))
TN = (((0,), (0,)), ((), ()))
F32 = jnp.float32
BF16 = jnp.bfloat16
MAXR = 3
BP = 2


EPS = 1e-06


def local(
    prelude_output, init_noise, core_weight, norm_gain, state_cotangent, step_counts, group_table
):
    full_width = core_weight.shape[1]
    local_width = core_weight.shape[0]
    slot_total = init_noise.shape[0]
    seq_length = init_noise.shape[1]
    row_count = slot_total * seq_length
    my_group = lax.axis_index("dp")
    column_first = lax.axis_index("mp") * local_width
    seq_total = group_table.shape[0]
    seq_index = jnp.arange(seq_total, dtype=jnp.int32)
    earlier = (group_table[:, None] == group_table[None, :]) & (
        seq_index[None, :] < seq_index[:, None]
    )
    slot_rank = jnp.sum(earlier.astype(jnp.int32), axis=1)
    selected_rows = (group_table[None, :] == my_group) & (
        slot_rank[None, :] == jnp.arange(slot_total, dtype=jnp.int32)[:, None]
    )
    slot_counts = jnp.sum(jnp.where(selected_rows, step_counts[None, :], 0), axis=1)
    chosen_weights = selected_rows.astype(jnp.bfloat16)
    injected_input = jnp.einsum(
        "br,ref->bef",
        chosen_weights,
        lax.all_gather(prelude_output, "dp", axis=0, tiled=True),
        preferred_element_type=jnp.float32,
    ).reshape(row_count, local_width)
    gain_local = lax.dynamic_slice_in_dim(norm_gain, column_first, local_width, 0)

    def feature_sum(values):
        return lax.psum(values, "mp")

    shard_state = init_noise.reshape(row_count, local_width)
    saved = []
    piece_rows = lax.all_gather(shard_state, "mp", axis=1, tiled=True)
    product = lax.dot_general(
        piece_rows, core_weight, (((1,), (1,)), ((), ())), preferred_element_type=jnp.float32
    )
    whole_state = piece_rows
    product, whole_state = (product, whole_state)
    for turn in range(MAXR):
        active = jnp.repeat(turn >= MAXR - slot_counts, seq_length)[:, None]
        if turn > 0:
            product = lax.dot_general(
                whole_state,
                core_weight,
                (((1,), (1,)), ((), ())),
                preferred_element_type=jnp.float32,
            )
        mixed = (product + injected_input).astype(jnp.bfloat16)
        mixed_float = mixed.astype(jnp.float32)
        if turn + 1 < MAXR:
            mixed_whole = lax.all_gather(mixed, "mp", axis=1, tiled=True).astype(jnp.float32)
            inverse_rms = lax.rsqrt(jnp.sum(mixed_whole * mixed_whole, axis=1) / full_width + EPS)
            renewed = (norm_gain * mixed_whole * inverse_rms[:, None]).astype(jnp.bfloat16)
            saved.append((whole_state, mixed_float, inverse_rms, active))
            whole_state = jnp.where(active, renewed, whole_state)
        else:
            inverse_rms = lax.rsqrt(
                feature_sum(jnp.sum(mixed_float * mixed_float, axis=1)) / full_width + EPS
            )
            saved.append((whole_state, mixed_float, inverse_rms, active))
    upstream = state_cotangent.reshape(row_count, local_width).astype(jnp.float32)
    weight_grad = jnp.zeros((local_width, full_width), jnp.float32)
    for back_index in range(BP):
        whole_state, mixed_float, inverse_rms, active = saved[MAXR - 1 - back_index]
        scaled = upstream * gain_local
        inner = feature_sum(jnp.sum(scaled * mixed_float, axis=1))
        delta = (
            inverse_rms[:, None] * scaled
            - mixed_float * (inverse_rms**3 * inner / full_width)[:, None]
        )
        delta_b = jnp.where(active, delta, 0.0).astype(jnp.bfloat16)
        weight_grad = weight_grad + lax.dot_general(
            delta_b, whole_state, (((0,), (0,)), ((), ())), preferred_element_type=jnp.float32
        )
        if back_index + 1 < BP:
            partial_rows = jnp.dot(delta_b, core_weight, preferred_element_type=jnp.float32)
            summed_rows = lax.psum_scatter(
                partial_rows.astype(jnp.bfloat16), "mp", scatter_dimension=1, tiled=True
            ).astype(jnp.float32)
            upstream = jnp.where(active, summed_rows, upstream)
    return lax.psum_scatter(
        weight_grad.astype(jnp.bfloat16), "dp", scatter_dimension=1, tiled=True
    ).astype(jnp.float32)


def core_kernel(
    n_dp, n_mp, full_width,
    pick_ref, own_ref, part_ref, prelude_ref, noise_ref, cot_ref, counts_ref, gain_ref, w_hbm,
    out_ref,
    w_ref, w8, u0, u1, u2, y0, y1, xs, ds, inject, acc, square, cot_rows, scaled, delta_b,
    pre_all, noise_all, cot_all, red, pair_send, pair_recv, line_send, line_recv,
    w_sem, in_send, in_recv, g_send, g_recv, x_send, x_recv, d_send, d_recv,
    red_send, red_recv, p_send, p_recv, l_send, l_recv,
):
    dp = lax.axis_index("dp")
    mp = lax.axis_index("mp")
    n_line = n_mp // 2
    line, side = mp // 2, lax.rem(mp, 2)
    blocks = n_mp // n_dp
    seq_dev, tokens, width = prelude_ref.shape
    rows = seq_dev * tokens

    w_copy = pltpu.make_async_copy(w_hbm, w_ref, w_sem)
    w_copy.start()

    barrier = pltpu.get_barrier_semaphore()
    for o in range(1, n_mp):
        pl.semaphore_signal(
            barrier, inc=1, device_id=(dp, lax.rem(mp + o, n_mp)), device_id_type=MESH
        )
    for o in range(1, n_dp):
        pl.semaphore_signal(
            barrier, inc=1, device_id=(lax.rem(dp + o, n_dp), mp), device_id_type=MESH
        )
    pl.semaphore_wait(barrier, n_mp + n_dp - 2)

    def remote(src, dst, send, recv, device):
        return pltpu.make_async_remote_copy(
            src_ref=src, dst_ref=dst, send_sem=send, recv_sem=recv,
            device_id=device, device_id_type=MESH,
        )

    in_copies = []
    for which, (src, dst) in enumerate(
        ((noise_ref.at[seq_dev], noise_all), (prelude_ref, pre_all), (cot_ref.at[seq_dev], cot_all))
    ):
        copies = []
        for o in range(1, n_dp):
            copy = remote(
                src, dst.at[dp], in_send.at[which, o], in_recv.at[which, o],
                (lax.rem(dp + o, n_dp), mp),
            )
            copy.start()
            copies.append(copy)
        in_copies.append(copies)
    noise_all[dp] = noise_ref[seq_dev]
    cot_all[dp] = cot_ref[seq_dev]
    pre_all[dp] = prelude_ref[...]

    def third_rows(own, gathered):
        total = own_ref[0] * own[seq_dev - 1].astype(F32)
        return lax.fori_loop(
            0, n_dp, lambda q, t: t + part_ref[q] * gathered[q].astype(F32), total
        )

    kept = (seq_dev - 1) * tokens
    for b in range(seq_dev - 1):
        u0[mp, pl.ds(b * tokens, tokens)] = noise_ref[b]
    for copy in in_copies[0]:
        copy.wait_recv()
    u0[mp, pl.ds(kept, tokens)] = third_rows(noise_ref, noise_all).astype(BF16)

    peer = (dp, line * 2 + 1 - side)

    def gather_start(turn, buf):
        own = buf.at[mp]
        remote(own, own, g_send.at[turn, 1], g_recv.at[turn, 1], peer).start()
        for h in range(1, n_line):
            to = (dp, lax.rem(line + h, n_line) * 2 + side)
            remote(own, own, g_send.at[turn, 1 + h], g_recv.at[turn, 1 + h], to).start()

    def gather_steps(turn, buf, use):
        def step(s, carry):
            h = jnp.where(s < 2, 0, jnp.where(s <= n_line, s - 1, s - n_line))
            other = jnp.where(s < 2, s, jnp.where(s <= n_line, 0, 1))
            from_line = lax.rem(line + n_line - h, n_line)
            owner = from_line * 2 + lax.rem(side + other, 2)

            @pl.when(s > 0)
            def _():
                remote(
                    buf.at[owner], buf.at[owner], g_send.at[turn, s], g_recv.at[turn, s], peer
                ).wait_recv()

            @pl.when((s >= 2) & (s <= n_line))
            def _():
                f = n_line + s - 1
                remote(
                    buf.at[owner], buf.at[owner], g_send.at[turn, f], g_recv.at[turn, f], peer
                ).start()

            use(owner)
            return carry

        lax.fori_loop(0, n_mp, step, 0)

    def gather_end(turn, buf):
        def step(s, carry):
            remote(
                buf.at[mp], buf.at[mp], g_send.at[turn, s], g_recv.at[turn, s], peer
            ).wait_send()
            return carry

        lax.fori_loop(1, n_mp, step, 0)

    gather_start(0, u0)
    w_copy.wait()
    for k in range(n_mp):
        w8[k] = w_ref[:, k * width : (k + 1) * width]

    counts = counts_ref[...]

    def active(turn):
        return counts >= float(MAXR - turn)

    acc[...] = jnp.zeros_like(acc)

    def use_first(k):
        acc[...] += lax.dot_general(u0[k], w8[k], NT, preferred_element_type=F32)

    gather_steps(0, u0, use_first)

    for copy in in_copies[1]:
        copy.wait_recv()
    for b in range(seq_dev):

        def add(q, t):
            for i in range(seq_dev):
                t = t + pick_ref[b * n_dp * seq_dev + q * seq_dev + i] * pre_all[q, i].astype(F32)
            return t

        inject[pl.ds(b * tokens, tokens)] = lax.fori_loop(
            0, n_dp, add, jnp.zeros((tokens, width), F32)
        )

    def renew(turn, y_all, before, after):
        live = active(turn)
        acc[...] = jnp.zeros_like(acc)
        square[...] = jnp.zeros_like(square)

        def use(k):
            y = y_all[k].astype(F32)
            square[...] += jnp.sum(y * y, axis=1, keepdims=True)
            new = jnp.where(live, gain_ref[k] * y, before[k].astype(F32)).astype(BF16)
            after[k] = new
            acc[...] += lax.dot_general(new, w8[k], NT, preferred_element_type=F32)
            to = k // blocks
            part = lax.rem(k, blocks)

            @pl.when(to == dp)
            def _():
                xs[turn, dp, part] = after[k]

            @pl.when(to != dp)
            def _():
                remote(
                    after.at[k], xs.at[turn, dp, part], x_send.at[turn, k],
                    x_recv.at[turn, dp, part], (to, mp),
                ).start()

        gather_steps(1 + turn, y_all, use)
        return lax.rsqrt(square[...] / full_width + EPS)

    y0[mp] = (acc[...] + inject[...]).astype(BF16)
    gather_start(1, y0)
    for copy in in_copies[2]:
        copy.wait_recv()
    cot_rows[pl.ds(kept, tokens)] = third_rows(cot_ref, cot_all)
    for b in range(seq_dev - 1):
        cot_rows[pl.ds(b * tokens, tokens)] = cot_ref[b].astype(F32)
    rms0 = renew(0, y0, u0, u1)
    scale1 = jnp.where(active(0), rms0, 1.0)

    y1[mp] = (scale1 * acc[...] + inject[...]).astype(BF16)
    gather_start(2, y1)
    rms1 = renew(1, y1, u1, u2)
    scale2 = jnp.where(active(1), rms1, scale1)
    y2 = (scale2 * acc[...] + inject[...]).astype(BF16).astype(F32)

    def all_sums(which, first, second):
        ones = jnp.ones((4, width), F32)

        def row_sum(values):
            return lax.dot_general(
                ones, values, NT, preferred_element_type=F32, precision=lax.Precision.HIGHEST
            )

        red[which, mp] = jnp.concatenate([row_sum(first), row_sum(second)], axis=0)
        copies = []
        for o in range(1, n_mp):
            copy = remote(
                red.at[which, mp], red.at[which, mp], red_send.at[which, o],
                red_recv.at[which, o], (dp, lax.rem(mp + o, n_mp)),
            )
            copy.start()
            copies.append(copy)
        for copy in copies:
            copy.wait_recv()
        total = red[which, 0]
        for k in range(1, n_mp):
            total = total + red[which, k]
        columns = jnp.transpose(total)
        return columns[:, 0:1], columns[:, 4:5], copies

    gain = gain_ref[mp]
    scaled[...] = cot_rows[...] * gain
    square2, inner2, copies_a = all_sums(0, y2 * y2, scaled[...] * y2)
    rms2 = lax.rsqrt(square2 / full_width + EPS)
    delta = jnp.where(
        active(2), rms2 * scaled[...] - y2 * (rms2 * rms2 * rms2 * inner2 / full_width), 0.0
    )
    delta_b[...] = delta.astype(BF16)

    def pair_step(s, carry):
        to_line = lax.rem(line + s + 1, n_line)
        product = jnp.dot(
            delta_b[...], w8[to_line * 2 + 1 - side], preferred_element_type=F32
        )
        pair_send[s] = product.astype(BF16)
        remote(pair_send.at[s], pair_recv.at[s], p_send.at[s], p_recv.at[s], peer).start()
        return carry

    lax.fori_loop(0, n_line, pair_step, 0)

    dp_pair, dp_side = dp // 2, lax.rem(dp, 2)
    n_pair = n_dp // 2
    dp_peer = (dp_pair * 2 + 1 - dp_side, mp)

    def spread_start(which, values):
        ds[which, dp] = values
        own = ds.at[which, dp]
        copies = []
        for h in range(1, n_pair):
            to = (lax.rem(dp_pair + h, n_pair) * 2 + dp_side, mp)
            copies.append(remote(own, own, d_send.at[which, h], d_recv.at[which, h], to))
        copies.append(remote(own, own, d_send.at[which, 0], d_recv.at[which, 0], dp_peer))
        for copy in copies:
            copy.start()
        return copies

    def spread_forward(which, copies):
        forwards = []
        for h in range(1, n_pair):
            copies[h - 1].wait_recv()
            held = ds.at[which, lax.rem(dp_pair + n_pair - h, n_pair) * 2 + dp_side]
            f = n_pair + h
            copy = remote(held, held, d_send.at[which, f], d_recv.at[which, f], dp_peer)
            copy.start()
            forwards.append(copy)
        return forwards

    def spread_wait(copies, forwards):
        copies[-1].wait_recv()
        for copy in forwards:
            copy.wait_recv()

    spread_a = spread_start(1, (delta * scale2).astype(BF16))

    def line_step(s, carry):
        to_line = lax.rem(line + s + 1, n_line)
        product = jnp.dot(delta_b[...], w8[to_line * 2 + side], preferred_element_type=F32)
        remote(
            pair_send.at[s], pair_recv.at[s], p_send.at[s], p_recv.at[s], peer
        ).wait_recv()
        total = product.astype(BF16).astype(F32) + pair_recv[s].astype(F32)
        acc[...] = total

        @pl.when(s < n_line - 1)
        def _():
            line_send[s] = total.astype(BF16)
            remote(
                line_send.at[s], line_recv.at[s], l_send.at[s], l_recv.at[s],
                (dp, to_line * 2 + side),
            ).start()

        return carry

    lax.fori_loop(0, n_line, line_step, 0)
    forwards_a = spread_forward(1, spread_a)

    def x_wait(which):
        for h in range(1, n_dp):
            q = lax.rem(dp + h, n_dp)
            for part in range(blocks):
                remote(
                    u1.at[0], xs.at[which, q, part], x_send.at[which, 0],
                    x_recv.at[which, q, part], (q, mp),
                ).wait_recv()

    def grad(which, part):
        left = ds[which].reshape(n_dp * rows, width)
        right = jnp.concatenate([xs[which, q, part] for q in range(n_dp)], axis=0)
        return lax.dot_general(left, right, TN, preferred_element_type=F32)

    spread_wait(spread_a, forwards_a)
    x_wait(1)
    for part in range(blocks):
        out_ref[:, part * width : (part + 1) * width] = grad(1, part)

    for s in range(n_line - 1):
        remote(
            line_send.at[s], line_recv.at[s], l_send.at[s], l_recv.at[s], peer
        ).wait_recv()
        acc[...] += line_recv[s].astype(F32)
    scaled[...] = jnp.where(active(2), acc[...], cot_rows[...]) * gain
    y_own = y1[mp].astype(F32)
    unused, inner1, copies_b = all_sums(1, y_own, scaled[...] * y_own)
    delta = jnp.where(
        active(1), rms1 * scaled[...] - y_own * (rms1 * rms1 * rms1 * inner1 / full_width), 0.0
    )
    spread_b = spread_start(0, (delta * scale1).astype(BF16))
    forwards_b = spread_forward(0, spread_b)
    x_wait(0)
    spread_wait(spread_b, forwards_b)
    for part in range(blocks):
        out_ref[:, part * width : (part + 1) * width] += grad(0, part)

    for copies in in_copies + [copies_a, copies_b, spread_a, forwards_a, spread_b, forwards_b]:
        for copy in copies:
            copy.wait_send()
    for turn, buf in enumerate((u0, y0, y1)):
        gather_end(turn, buf)
    for s in range(n_line):
        remote(
            pair_send.at[s], pair_recv.at[s], p_send.at[s], p_recv.at[s], peer
        ).wait_send()
    for s in range(n_line - 1):
        remote(
            line_send.at[s], line_recv.at[s], l_send.at[s], l_recv.at[s], peer
        ).wait_send()
    for turn, buf in enumerate((u1, u2)):
        for h in range(1, n_dp):
            q = lax.rem(dp + h, n_dp)
            for part in range(blocks):
                k = q * blocks + part
                remote(
                    buf.at[k], xs.at[turn, dp, part], x_send.at[turn, k],
                    x_recv.at[turn, dp, part], (q, mp),
                ).wait_send()


def fused(
    n_dp, n_mp,
    prelude_output, init_noise, core_weight, norm_gain, state_cotangent, step_counts, group_table,
):
    width, full_width = core_weight.shape
    seq_dev, tokens = prelude_output.shape[:2]
    cap = init_noise.shape[0]
    rows = seq_dev * tokens
    blocks = n_mp // n_dp
    dp = lax.axis_index("dp")
    seqs = group_table.shape[0]
    index = jnp.arange(seqs, dtype=jnp.int32)
    groups = jnp.arange(n_dp, dtype=jnp.int32)
    same = group_table[:, None] == group_table[None, :]
    rank = jnp.sum((same & (index[None, :] < index[:, None])).astype(jnp.int32), axis=1)
    sizes = jnp.sum((group_table[None, :] == groups[:, None]).astype(jnp.int32), axis=1)
    full = sizes == cap
    mine_full = jnp.sum(jnp.where(groups == dp, full, False).astype(jnp.int32)) > 0
    earlier = groups[None, :] < groups[:, None]
    order = jnp.sum((earlier & (full[None, :] == full[:, None])).astype(jnp.int32), axis=1)
    mine_order = jnp.sum(jnp.where(groups == dp, order, 0))
    part = full & (order == mine_order) & ~mine_full
    partner = jnp.sum(jnp.where(part, groups, 0))
    place = jnp.arange(seq_dev, dtype=jnp.int32)
    moved = (place == seq_dev - 1) & ~mine_full
    want_group = jnp.where(moved, partner, dp)
    want_rank = jnp.where(moved, cap - 1, place)
    pick = (group_table[None, :] == want_group[:, None]) & (rank[None, :] == want_rank[:, None])
    counts = jnp.sum(jnp.where(pick, step_counts[None, :], 0), axis=1)
    row_counts = jnp.repeat(counts.astype(F32), tokens)[:, None]
    vmem = pl.BlockSpec(memory_space=pltpu.VMEM)
    smem = pl.BlockSpec(memory_space=pltpu.SMEM)
    state = pltpu.VMEM((n_mp, rows, width), BF16)
    row_f32 = pltpu.VMEM((rows, width), F32)
    n_line, n_pair = n_mp // 2, n_dp // 2
    dma = pltpu.SemaphoreType.DMA
    scratch = [
        pltpu.VMEM((width, full_width), BF16),
        pltpu.VMEM((n_mp, width, width), BF16),
        state, state, state, state, state,
        pltpu.VMEM((BP, n_dp, blocks, rows, width), BF16),
        pltpu.VMEM((BP, n_dp, rows, width), BF16),
        row_f32, row_f32, pltpu.VMEM((rows, 1), F32), row_f32, row_f32,
        pltpu.VMEM((rows, width), BF16),
        pltpu.VMEM((n_dp, seq_dev, tokens, width), BF16),
        pltpu.VMEM((n_dp, tokens, width), BF16),
        pltpu.VMEM((n_dp, tokens, width), BF16),
        pltpu.VMEM((BP, n_mp, 8, rows), F32),
        pltpu.VMEM((n_line, rows, width), BF16),
        pltpu.VMEM((n_line, rows, width), BF16),
        pltpu.VMEM((n_line, rows, width), BF16),
        pltpu.VMEM((n_line, rows, width), BF16),
        dma,
        dma((3, n_dp)), dma((3, n_dp)),
        dma((MAXR, n_mp)), dma((MAXR, n_mp)),
        dma((BP, n_mp)), dma((BP, n_dp, blocks)),
        dma((BP, 2 * n_pair)), dma((BP, 2 * n_pair)),
        dma((BP, n_mp)), dma((BP, n_mp)),
        dma((n_line,)), dma((n_line,)),
        dma((n_line,)), dma((n_line,)),
    ]
    return pl.pallas_call(
        functools.partial(core_kernel, n_dp, n_mp, full_width),
        out_shape=jax.ShapeDtypeStruct((width, blocks * width), F32),
        in_specs=[smem] * 3 + [vmem] * 5 + [pl.BlockSpec(memory_space=pl.ANY)],
        out_specs=vmem,
        scratch_shapes=scratch,
        compiler_params=pltpu.CompilerParams(
            collective_id=0, has_side_effects=True, vmem_limit_bytes=56 * 1024 * 1024
        ),
        cost_estimate=pl.CostEstimate(
            flops=2 * rows * full_width * width * 8, bytes_accessed=20_000_000, transcendentals=0
        ),
    )(
        pick.astype(F32).reshape(-1),
        mine_full.astype(F32).reshape(1),
        part.astype(F32),
        prelude_output,
        init_noise,
        state_cotangent,
        row_counts,
        norm_gain.reshape(n_mp, 1, width),
        core_weight,
    )


def solution(mesh):
    n_dp, n_mp = mesh.shape["dp"], mesh.shape["mp"]
    paired = n_mp % n_dp == 0 and n_mp % 2 == 0 and n_dp % 2 == 0
    return jax.shard_map(
        functools.partial(fused, n_dp, n_mp) if paired else local,
        mesh=mesh,
        in_specs=(
            P("dp", None, "mp"),
            P("dp", None, "mp"),
            P("mp", None),
            P(),
            P("dp", None, "mp"),
            P(),
            P(),
        ),
        out_specs=P("mp", "dp"),
        check_vma=False,
    )
```

```python
import functools

import jax
import jax.numpy as jnp
from jax import lax
from jax.experimental import pallas as pl
from jax.experimental.pallas import tpu as pltpu
from jax.sharding import PartitionSpec as P

MESH = pl.DeviceIdType.MESH
NT = (((1,), (1,)), ((), ()))
TN = (((0,), (0,)), ((), ()))
STREAMS = 2
F32 = jnp.float32
BF16 = jnp.bfloat16
MAXR = 3
BP = 2


EPS = 1e-06


def local(
    prelude_output, init_noise, core_weight, norm_gain, state_cotangent, step_counts, group_table
):
    full_width = core_weight.shape[1]
    local_width = core_weight.shape[0]
    slot_total = init_noise.shape[0]
    seq_length = init_noise.shape[1]
    row_count = slot_total * seq_length
    my_group = lax.axis_index("dp")
    column_first = lax.axis_index("mp") * local_width
    seq_total = group_table.shape[0]
    seq_index = jnp.arange(seq_total, dtype=jnp.int32)
    earlier = (group_table[:, None] == group_table[None, :]) & (
        seq_index[None, :] < seq_index[:, None]
    )
    slot_rank = jnp.sum(earlier.astype(jnp.int32), axis=1)
    selected_rows = (group_table[None, :] == my_group) & (
        slot_rank[None, :] == jnp.arange(slot_total, dtype=jnp.int32)[:, None]
    )
    slot_counts = jnp.sum(jnp.where(selected_rows, step_counts[None, :], 0), axis=1)
    chosen_weights = selected_rows.astype(jnp.bfloat16)
    injected_input = jnp.einsum(
        "br,ref->bef",
        chosen_weights,
        lax.all_gather(prelude_output, "dp", axis=0, tiled=True),
        preferred_element_type=jnp.float32,
    ).reshape(row_count, local_width)
    gain_local = lax.dynamic_slice_in_dim(norm_gain, column_first, local_width, 0)

    def feature_sum(values):
        return lax.psum(values, "mp")

    shard_state = init_noise.reshape(row_count, local_width)
    saved = []
    piece_rows = lax.all_gather(shard_state, "mp", axis=1, tiled=True)
    product = lax.dot_general(
        piece_rows, core_weight, (((1,), (1,)), ((), ())), preferred_element_type=jnp.float32
    )
    whole_state = piece_rows
    product, whole_state = (product, whole_state)
    for turn in range(MAXR):
        active = jnp.repeat(turn >= MAXR - slot_counts, seq_length)[:, None]
        if turn > 0:
            product = lax.dot_general(
                whole_state,
                core_weight,
                (((1,), (1,)), ((), ())),
                preferred_element_type=jnp.float32,
            )
        mixed = (product + injected_input).astype(jnp.bfloat16)
        mixed_float = mixed.astype(jnp.float32)
        if turn + 1 < MAXR:
            mixed_whole = lax.all_gather(mixed, "mp", axis=1, tiled=True).astype(jnp.float32)
            inverse_rms = lax.rsqrt(jnp.sum(mixed_whole * mixed_whole, axis=1) / full_width + EPS)
            renewed = (norm_gain * mixed_whole * inverse_rms[:, None]).astype(jnp.bfloat16)
            saved.append((whole_state, mixed_float, inverse_rms, active))
            whole_state = jnp.where(active, renewed, whole_state)
        else:
            inverse_rms = lax.rsqrt(
                feature_sum(jnp.sum(mixed_float * mixed_float, axis=1)) / full_width + EPS
            )
            saved.append((whole_state, mixed_float, inverse_rms, active))
    upstream = state_cotangent.reshape(row_count, local_width).astype(jnp.float32)
    weight_grad = jnp.zeros((local_width, full_width), jnp.float32)
    for back_index in range(BP):
        whole_state, mixed_float, inverse_rms, active = saved[MAXR - 1 - back_index]
        scaled = upstream * gain_local
        inner = feature_sum(jnp.sum(scaled * mixed_float, axis=1))
        delta = (
            inverse_rms[:, None] * scaled
            - mixed_float * (inverse_rms**3 * inner / full_width)[:, None]
        )
        delta_b = jnp.where(active, delta, 0.0).astype(jnp.bfloat16)
        weight_grad = weight_grad + lax.dot_general(
            delta_b, whole_state, (((0,), (0,)), ((), ())), preferred_element_type=jnp.float32
        )
        if back_index + 1 < BP:
            partial_rows = jnp.dot(delta_b, core_weight, preferred_element_type=jnp.float32)
            summed_rows = lax.psum_scatter(
                partial_rows.astype(jnp.bfloat16), "mp", scatter_dimension=1, tiled=True
            ).astype(jnp.float32)
            upstream = jnp.where(active, summed_rows, upstream)
    return lax.psum_scatter(
        weight_grad.astype(jnp.bfloat16), "dp", scatter_dimension=1, tiled=True
    ).astype(jnp.float32)


def core_kernel(
    n_dp, n_mp, streams, full_width, cap,
    counts_in, groups_in, prelude_ref, noise_ref, cot_ref, gain_in, w_hbm,
    ds, xs,
    w_ref, w8, u0, u1, u2, y0, y1, gain_ref, counts_ref, pick_ref, inject, acc, square, scale, rms,
    cot_rows, scaled, y_last, delta_b, spread_own, total_ref, noise_rows,
    pre_all, noise_all, cot_all, red, pair_send, pair_recv, line_send, line_recv,
    w_sem, in_send, in_recv, g_send, g_recv, x_send, x_recv, own_sem, d_send, d_recv,
    red_send, red_recv, p_send, p_recv, l_send, l_recv,
):
    dp = lax.axis_index("dp")
    mp = lax.axis_index("mp")
    n_line = n_mp // 2
    line, side = mp // 2, lax.rem(mp, 2)
    blocks = n_mp // n_dp
    seq_dev, tokens, width = prelude_ref.shape
    rows = seq_dev * tokens
    part_rows = rows // streams

    w_copy = pltpu.make_async_copy(w_hbm, w_ref, w_sem)
    w_copy.start()

    barrier = pltpu.get_barrier_semaphore()
    for o in range(1, n_mp):
        pl.semaphore_signal(
            barrier, inc=1, device_id=(dp, lax.rem(mp + o, n_mp)), device_id_type=MESH
        )
    for o in range(1, n_dp):
        pl.semaphore_signal(
            barrier, inc=1, device_id=(lax.rem(dp + o, n_dp), mp), device_id_type=MESH
        )

    seqs = groups_in.shape[0]
    one, zero = jnp.int32(1), jnp.int32(0)
    group = [groups_in[i] for i in range(seqs)]
    rank = []
    for i in range(seqs):
        r = zero
        for j in range(i):
            r = r + jnp.where(group[j] == group[i], one, zero)
        rank.append(r)
    full = []
    for g in range(n_dp):
        size = zero
        for i in range(seqs):
            size = size + jnp.where(group[i] == g, one, zero)
        full.append(jnp.where(size == cap, one, zero))
    order = []
    for g in range(n_dp):
        r = zero
        for e in range(g):
            r = r + jnp.where(full[e] == full[g], one, zero)
        order.append(r)
    mine_full, mine_order = zero, zero
    for g in range(n_dp):
        mine_full = jnp.where(dp == g, full[g], mine_full)
        mine_order = jnp.where(dp == g, order[g], mine_order)
    partner = zero
    part_weight = []
    for g in range(n_dp):
        hit = full[g] * (one - mine_full) * jnp.where(order[g] == mine_order, one, zero)
        partner = partner + hit * g
        part_weight.append(hit.astype(F32))
    own_weight = mine_full.astype(F32)
    for b in range(seq_dev):
        want_group, want_rank = dp, jnp.int32(b)
        if b == seq_dev - 1:
            want_group = jnp.where(mine_full == one, dp, partner)
            want_rank = jnp.where(mine_full == one, want_rank, cap - 1)
        count = zero
        for i in range(seqs):
            hit = jnp.where(group[i] == want_group, one, zero) * jnp.where(
                rank[i] == want_rank, one, zero
            )
            count = count + hit * counts_in[i]
            pick_ref[b * seqs + i] = hit.astype(F32)
        counts_ref[pl.ds(b * tokens, tokens)] = jnp.zeros((tokens, 1), F32) + count.astype(F32)

    pl.semaphore_wait(barrier, n_mp + n_dp - 2)

    def remote(src, dst, send, recv, device):
        return pltpu.make_async_remote_copy(
            src_ref=src, dst_ref=dst, send_sem=send, recv_sem=recv,
            device_id=device, device_id_type=MESH,
        )

    in_copies = []

    def cross(which, src, dst):
        copies = []
        for o in range(1, n_dp):
            copy = remote(
                src, dst.at[dp], in_send.at[which, o], in_recv.at[which, o],
                (lax.rem(dp + o, n_dp), mp),
            )
            copy.start()
            copies.append(copy)
        in_copies.append(copies)

    cross(0, noise_ref.at[seq_dev], noise_all)
    peer = (dp, line * 2 + 1 - side)

    def gather_start(turn, s, buf):
        own = buf.at[s, mp]
        remote(own, own, g_send.at[turn, s, 1], g_recv.at[turn, s, 1], peer).start()
        for h in range(1, n_line):
            to = (dp, lax.rem(line + h, n_line) * 2 + side)
            remote(own, own, g_send.at[turn, s, 1 + h], g_recv.at[turn, s, 1 + h], to).start()

    def gather_wait(turn, s, buf, at, owner):
        remote(
            buf.at[s, owner], buf.at[s, owner], g_send.at[turn, s, at], g_recv.at[turn, s, at], peer
        ).wait_recv()

    def gather_forward(turn, s, buf, h):
        owner = lax.rem(line + n_line - h, n_line) * 2 + side
        gather_wait(turn, s, buf, 1 + h, owner)
        at = n_line + h
        remote(
            buf.at[s, owner], buf.at[s, owner], g_send.at[turn, s, at], g_recv.at[turn, s, at], peer
        ).start()

    def gather_steps(turn, s, buf, use, forwarded=False):
        def step(at, carry):
            h = jnp.where(at < 2, 0, jnp.where(at <= n_line, at - 1, at - n_line))
            other = jnp.where(at < 2, at, jnp.where(at <= n_line, 0, 1))
            owner = lax.rem(line + n_line - h, n_line) * 2 + lax.rem(side + other, 2)

            @pl.when((at == 1) | (at > n_line))
            def _():
                gather_wait(turn, s, buf, at, owner)

            if not forwarded:

                @pl.when((at >= 2) & (at <= n_line))
                def _():
                    gather_forward(turn, s, buf, h)

            use(owner)
            return carry

        lax.fori_loop(0, n_mp, step, 0)

    def each_stream(body):
        def step(s, carry):
            body(s)
            return carry

        lax.fori_loop(0, streams, step, 0)

    def third_rows(own, gathered):
        total = own_weight * own[seq_dev - 1].astype(F32)
        for q in range(n_dp):
            total = total + part_weight[q] * gathered[q].astype(F32)
        return total

    kept = (seq_dev - 1) * tokens
    for b in range(seq_dev - 1):
        noise_rows[pl.ds(b * tokens, tokens)] = noise_ref[b]
    ready = kept // part_rows

    def first_start(s):
        u0[s, mp] = noise_rows[pl.ds(s * part_rows, part_rows)]
        gather_start(0, s, u0)

    for s in range(ready):
        first_start(s)
    noise_all[dp] = noise_ref[seq_dev]
    for copy in in_copies[0]:
        copy.wait_recv()
    noise_rows[pl.ds(kept, tokens)] = third_rows(noise_ref, noise_all).astype(BF16)
    for s in range(ready, streams):
        first_start(s)
    cross(1, prelude_ref, pre_all)
    cross(2, cot_ref.at[seq_dev], cot_all)
    pre_all[dp] = prelude_ref[...]
    cot_all[dp] = cot_ref[seq_dev]

    w_copy.wait()
    waiting = [(s, h) for s in range(streams) for h in range(1, n_line)]
    for k in range(n_mp):
        w8[k] = w_ref[:, k * width : (k + 1) * width]
        gain_ref[k] = gain_in[:, k * width : (k + 1) * width]
        take = -(-len(waiting) // (n_mp - k))
        for s, h in waiting[:take]:
            gather_forward(0, s, u0, h)
        waiting = waiting[take:]

    for copy in in_copies[1]:
        copy.wait_recv()
    for b in range(seq_dev):

        def add(q, t, b=b):
            for i in range(seq_dev):
                t = t + pick_ref[b * seqs + q * seq_dev + i] * pre_all[q, i].astype(F32)
            return t

        inject[pl.ds(b * tokens, tokens)] = lax.fori_loop(
            0, n_dp, add, jnp.zeros((tokens, width), F32)
        )

    def rows_of(s):
        return pl.ds(pl.multiple_of(s * part_rows, part_rows), part_rows)

    def active(turn, s):
        return counts_ref[rows_of(s)] >= float(MAXR - turn)

    def first(s):
        acc[s] = jnp.zeros((part_rows, width), F32)

        def use(k):
            acc[s] += lax.dot_general(u0[s, k], w8[k], NT, preferred_element_type=F32)

        gather_steps(0, s, u0, use, forwarded=True)
        y0[s, mp] = (acc[s] + inject[rows_of(s)]).astype(BF16)
        gather_start(1, s, y0)

    each_stream(first)

    def renew(turn, s, y_all, before, after):
        live = active(turn, s)
        acc[s] = jnp.zeros((part_rows, width), F32)
        square[...] = jnp.zeros_like(square)

        def use(k):
            y = y_all[s, k].astype(F32)
            square[...] += jnp.sum(y * y, axis=1, keepdims=True)
            new = jnp.where(live, gain_ref[k] * y, before[s, k].astype(F32)).astype(BF16)
            after[s, k] = new
            acc[s] += lax.dot_general(new, w8[k], NT, preferred_element_type=F32)
            to = k // blocks
            part = lax.rem(k, blocks)
            dst = xs.at[part, turn, s, dp]

            @pl.when(to == dp)
            def _():
                pltpu.make_async_copy(after.at[s, k], dst, own_sem.at[turn, s, part]).start()

            @pl.when(to != dp)
            def _():
                remote(
                    after.at[s, k], dst, x_send.at[turn, s, k], x_recv.at[turn, s, dp, part],
                    (to, mp),
                ).start()

        gather_steps(1 + turn, s, y_all, use)
        root = lax.rsqrt(square[...] / full_width + EPS)
        rms[turn, rows_of(s)] = root
        previous = 1.0 if turn == 0 else scale[turn - 1, rows_of(s)]
        scale[turn, rows_of(s)] = jnp.where(live, root, previous)

    def second(s):
        renew(0, s, y0, u0, u1)
        y1[s, mp] = (scale[0, rows_of(s)] * acc[s] + inject[rows_of(s)]).astype(BF16)
        gather_start(2, s, y1)

    each_stream(second)

    for copy in in_copies[2]:
        copy.wait_recv()
    gain = gain_ref[mp]
    cot_rows[pl.ds(kept, tokens)] = third_rows(cot_ref, cot_all)
    for b in range(seq_dev - 1):
        cot_rows[pl.ds(b * tokens, tokens)] = cot_ref[b].astype(F32)
    scaled[...] = cot_rows[...] * gain

    def sums_start(which, s, values):
        ones = jnp.ones((4, width), F32)
        lines = [
            lax.dot_general(
                ones, v, NT, preferred_element_type=F32, precision=lax.Precision.HIGHEST
            )
            for v in values
        ]
        red[which, s, mp] = jnp.concatenate(lines, axis=0)
        own = red.at[which, s, mp]
        for o in range(1, n_mp):
            remote(
                own, own, red_send.at[which, s, o], red_recv.at[which, s, o],
                (dp, lax.rem(mp + o, n_mp)),
            ).start()

    def sums_end(which, s):
        own = red.at[which, s, mp]
        for o in range(1, n_mp):
            remote(
                own, own, red_send.at[which, s, o], red_recv.at[which, s, o], peer
            ).wait_recv()
        total = red[which, s, 0]
        for k in range(1, n_mp):
            total = total + red[which, s, k]
        columns = jnp.transpose(total)
        return columns[:, 0:1], columns[:, 4:5]

    def third(s):
        renew(1, s, y1, u1, u2)
        y = (scale[1, rows_of(s)] * acc[s] + inject[rows_of(s)]).astype(BF16).astype(F32)
        y_last[rows_of(s)] = y
        sums_start(0, s, (y * y, scaled[rows_of(s)] * y))

    each_stream(third)

    dp_pair, dp_side = dp // 2, lax.rem(dp, 2)
    n_pair = n_dp // 2
    dp_peer = (dp_pair * 2 + 1 - dp_side, mp)

    def spread_copies(which, s):
        own, dst = spread_own.at[which, s], ds.at[which, s, dp]
        copies = []
        for h in range(1, n_pair):
            to = (lax.rem(dp_pair + h, n_pair) * 2 + dp_side, mp)
            copies.append(remote(own, dst, d_send.at[which, s, h], d_recv.at[which, s, h], to))
        copies.append(remote(own, dst, d_send.at[which, s, 0], d_recv.at[which, s, 0], dp_peer))
        return copies, pltpu.make_async_copy(own, dst, own_sem.at[which, s, blocks])

    def spread_start(which, s, values):
        spread_own[which, s] = values
        copies, local_copy = spread_copies(which, s)
        for copy in copies:
            copy.start()
        local_copy.start()

    def spread_forwards(which, s):
        forwards = []
        for h in range(1, n_pair):
            held = ds.at[which, s, lax.rem(dp_pair + n_pair - h, n_pair) * 2 + dp_side]
            f = n_pair + h
            forwards.append(
                remote(held, held, d_send.at[which, s, f], d_recv.at[which, s, f], dp_peer)
            )
        return forwards

    def spread_forward(which, s):
        copies, unused = spread_copies(which, s)
        for copy, forward in zip(copies, spread_forwards(which, s)):
            copy.wait_recv()
            forward.start()

    def pair_copy(s, at):
        return remote(
            pair_send.at[s, at], pair_recv.at[s, at], p_send.at[s, at], p_recv.at[s, at], peer
        )

    def line_copy(s, at):
        to = (dp, lax.rem(line + at + 1, n_line) * 2 + side)
        return remote(
            line_send.at[s, at], line_recv.at[s, at], l_send.at[s, at], l_recv.at[s, at], to
        )

    def back_first(s):
        square2, inner2 = sums_end(0, s)
        root = lax.rsqrt(square2 / full_width + EPS)
        y = y_last[rows_of(s)]
        delta = jnp.where(
            active(2, s),
            root * scaled[rows_of(s)] - y * (root * root * root * inner2 / full_width),
            0.0,
        )
        delta_b[s] = delta.astype(BF16)

        def pair_step(at, carry):
            to_line = lax.rem(line + at + 1, n_line)
            product = jnp.dot(
                delta_b[s], w8[to_line * 2 + 1 - side], preferred_element_type=F32
            )
            pair_send[s, at] = product.astype(BF16)
            pair_copy(s, at).start()
            return carry

        lax.fori_loop(0, n_line, pair_step, 0)
        spread_start(1, s, (delta * scale[1, rows_of(s)]).astype(BF16))
        inner = delta_b[s].astype(F32) * acc[s]
        sums_start(1, s, (inner, inner))

    each_stream(back_first)

    def back_second(s):
        def line_step(at, carry):
            to_line = lax.rem(line + at + 1, n_line)
            product = jnp.dot(delta_b[s], w8[to_line * 2 + side], preferred_element_type=F32)
            pair_copy(s, at).wait_recv()
            total = product.astype(BF16).astype(F32) + pair_recv[s, at].astype(F32)
            total_ref[s] = total

            @pl.when(at < n_line - 1)
            def _():
                line_send[s, at] = total.astype(BF16)
                line_copy(s, at).start()

            return carry

        lax.fori_loop(0, n_line, line_step, 0)

    each_stream(back_second)
    for s in range(streams):
        spread_forward(1, s)

    def back_third(s):
        unused, inner = sums_end(1, s)
        total = total_ref[s]
        for at in range(n_line - 1):
            line_copy(s, at).wait_recv()
            total = total + line_recv[s, at].astype(F32)
        upstream = jnp.where(active(2, s), total, cot_rows[rows_of(s)])
        y = y1[s, mp].astype(F32)
        root = rms[1, rows_of(s)]
        delta = jnp.where(
            active(1, s),
            root * (upstream * gain) - y * (root * root * root * inner / full_width),
            0.0,
        )
        spread_start(0, s, (delta * scale[0, rows_of(s)]).astype(BF16))

    each_stream(back_third)
    for s in range(streams):
        spread_forward(0, s)

    def finish(s):
        for which in range(BP):
            copies, local_copy = spread_copies(which, s)
            copies[-1].wait_recv()
            for copy in spread_forwards(which, s):
                copy.wait()
            for copy in copies:
                copy.wait_send()
            local_copy.wait()
            for part in range(blocks):
                pltpu.make_async_copy(
                    u1.at[s, 0], xs.at[part, which, s, dp], own_sem.at[which, s, part]
                ).wait()
                for h in range(1, n_dp):
                    q = lax.rem(dp + h, n_dp)
                    copy = remote(
                        u1.at[s, 0], xs.at[part, which, s, q],
                        x_send.at[which, s, q * blocks + part], x_recv.at[which, s, q, part],
                        (q, mp),
                    )
                    copy.wait()
            own = red.at[which, s, mp]
            for o in range(1, n_mp):
                remote(
                    own, own, red_send.at[which, s, o], red_recv.at[which, s, o], peer
                ).wait_send()
        for turn, buf in enumerate((u0, y0, y1)):
            for at in range(1, n_mp):
                remote(
                    buf.at[s, mp], buf.at[s, mp], g_send.at[turn, s, at], g_recv.at[turn, s, at],
                    peer,
                ).wait_send()
        for at in range(n_line):
            pair_copy(s, at).wait_send()
        for at in range(n_line - 1):
            line_copy(s, at).wait_send()

    each_stream(finish)
    for copies in in_copies:
        for copy in copies:
            copy.wait_send()


def grad_kernel(ds_ref, xs_ref, out_ref):
    width = ds_ref.shape[-1]
    left = ds_ref[...].reshape(-1, width)
    depth = left.shape[0]
    full = xs_ref.shape[-1]
    for part in range(xs_ref.shape[0]):
        right = xs_ref[part].reshape(depth, full)
        out_ref[:, part * full : (part + 1) * full] = lax.dot_general(
            left, right, TN, preferred_element_type=F32
        )


def fused(
    n_dp, n_mp, streams,
    prelude_output, init_noise, core_weight, norm_gain, state_cotangent, step_counts, group_table,
):
    width, full_width = core_weight.shape
    seq_dev, tokens = prelude_output.shape[:2]
    cap = init_noise.shape[0]
    seqs = group_table.shape[0]
    rows = seq_dev * tokens
    part_rows = rows // streams
    blocks = n_mp // n_dp
    n_line, n_pair = n_mp // 2, n_dp // 2
    vmem = pl.BlockSpec(memory_space=pltpu.VMEM)
    smem = pl.BlockSpec(memory_space=pltpu.SMEM)
    any_space = pl.BlockSpec(memory_space=pl.ANY)
    state = pltpu.VMEM((streams, n_mp, part_rows, width), BF16)
    row_f32 = pltpu.VMEM((rows, width), F32)
    stream_f32 = pltpu.VMEM((streams, part_rows, width), F32)
    pieces = pltpu.VMEM((streams, n_line, part_rows, width), BF16)
    dma = pltpu.SemaphoreType.DMA
    scratch = [
        pltpu.VMEM((width, full_width), BF16),
        pltpu.VMEM((n_mp, width, width), BF16),
        state, state, state, state, state,
        pltpu.VMEM((n_mp, 1, width), F32),
        pltpu.VMEM((rows, 1), F32),
        pltpu.SMEM((seq_dev * seqs,), F32),
        row_f32, stream_f32,
        pltpu.VMEM((part_rows, 1), F32),
        pltpu.VMEM((BP, rows, 1), F32),
        pltpu.VMEM((BP, rows, 1), F32),
        row_f32, row_f32, row_f32,
        pltpu.VMEM((streams, part_rows, width), BF16),
        pltpu.VMEM((BP, streams, part_rows, width), BF16),
        stream_f32,
        pltpu.VMEM((rows, width), BF16),
        pltpu.VMEM((n_dp, seq_dev, tokens, width), BF16),
        pltpu.VMEM((n_dp, tokens, width), BF16),
        pltpu.VMEM((n_dp, tokens, width), BF16),
        pltpu.VMEM((BP, streams, n_mp, 8, part_rows), F32),
        pieces, pieces, pieces, pieces,
        dma,
        dma((3, n_dp)), dma((3, n_dp)),
        dma((MAXR, streams, n_mp)), dma((MAXR, streams, n_mp)),
        dma((BP, streams, n_mp)), dma((BP, streams, n_dp, blocks)),
        dma((BP, streams, blocks + 1)),
        dma((BP, streams, 2 * n_pair)), dma((BP, streams, 2 * n_pair)),
        dma((BP, streams, n_mp)), dma((BP, streams, n_mp)),
        dma((streams, n_line)), dma((streams, n_line)),
        dma((streams, n_line)), dma((streams, n_line)),
    ]
    deltas, states = pl.pallas_call(
        functools.partial(core_kernel, n_dp, n_mp, streams, full_width, cap),
        out_shape=(
            jax.ShapeDtypeStruct((BP, streams, n_dp, part_rows, width), BF16),
            jax.ShapeDtypeStruct((blocks, BP, streams, n_dp, part_rows, width), BF16),
        ),
        in_specs=[smem] * 2 + [vmem] * 4 + [any_space],
        out_specs=(any_space, any_space),
        scratch_shapes=scratch,
        compiler_params=pltpu.CompilerParams(
            collective_id=0, has_side_effects=True, vmem_limit_bytes=56 * 1024 * 1024
        ),
        cost_estimate=pl.CostEstimate(
            flops=2 * rows * full_width * width * 4, bytes_accessed=20_000_000, transcendentals=0
        ),
    )(
        step_counts, group_table, prelude_output, init_noise, state_cotangent,
        norm_gain.reshape(1, full_width), core_weight,
    )
    tile = 256
    return pl.pallas_call(
        grad_kernel,
        grid=(pl.cdiv(width, tile),),
        out_shape=jax.ShapeDtypeStruct((width, blocks * width), F32),
        in_specs=[
            pl.BlockSpec((BP, streams, n_dp, part_rows, tile), lambda i: (0, 0, 0, 0, i)),
            pl.BlockSpec(states.shape, lambda i: (0,) * 6),
        ],
        out_specs=pl.BlockSpec((tile, blocks * width), lambda i: (i, 0)),
        compiler_params=pltpu.CompilerParams(vmem_limit_bytes=48 * 1024 * 1024),
    )(deltas, states)


def solution(mesh):
    n_dp, n_mp = mesh.shape["dp"], mesh.shape["mp"]
    paired = n_mp % n_dp == 0 and n_mp % 2 == 0 and n_dp % 2 == 0
    return jax.shard_map(
        functools.partial(fused, n_dp, n_mp, STREAMS) if paired else local,
        mesh=mesh,
        in_specs=(
            P("dp", None, "mp"),
            P("dp", None, "mp"),
            P("mp", None),
            P(),
            P("dp", None, "mp"),
            P(),
            P(),
        ),
        out_specs=P("mp", "dp"),
        check_vma=False,
    )
```

```python
import functools

import jax
import jax.numpy as jnp
from jax import lax
from jax.experimental import pallas as pl
from jax.experimental.pallas import tpu as pltpu
from jax.sharding import PartitionSpec as P

MESH = pl.DeviceIdType.MESH
NT = (((1,), (1,)), ((), ()))
TN = (((0,), (0,)), ((), ()))
STREAMS = 3
F32 = jnp.float32
BF16 = jnp.bfloat16
MAXR = 3
BP = 2


EPS = 1e-06


def local(
    prelude_output, init_noise, core_weight, norm_gain, state_cotangent, step_counts, group_table
):
    full_width = core_weight.shape[1]
    local_width = core_weight.shape[0]
    slot_total = init_noise.shape[0]
    seq_length = init_noise.shape[1]
    row_count = slot_total * seq_length
    my_group = lax.axis_index("dp")
    column_first = lax.axis_index("mp") * local_width
    seq_total = group_table.shape[0]
    seq_index = jnp.arange(seq_total, dtype=jnp.int32)
    earlier = (group_table[:, None] == group_table[None, :]) & (
        seq_index[None, :] < seq_index[:, None]
    )
    slot_rank = jnp.sum(earlier.astype(jnp.int32), axis=1)
    selected_rows = (group_table[None, :] == my_group) & (
        slot_rank[None, :] == jnp.arange(slot_total, dtype=jnp.int32)[:, None]
    )
    slot_counts = jnp.sum(jnp.where(selected_rows, step_counts[None, :], 0), axis=1)
    chosen_weights = selected_rows.astype(jnp.bfloat16)
    injected_input = jnp.einsum(
        "br,ref->bef",
        chosen_weights,
        lax.all_gather(prelude_output, "dp", axis=0, tiled=True),
        preferred_element_type=jnp.float32,
    ).reshape(row_count, local_width)
    gain_local = lax.dynamic_slice_in_dim(norm_gain, column_first, local_width, 0)

    def feature_sum(values):
        return lax.psum(values, "mp")

    shard_state = init_noise.reshape(row_count, local_width)
    saved = []
    piece_rows = lax.all_gather(shard_state, "mp", axis=1, tiled=True)
    product = lax.dot_general(
        piece_rows, core_weight, (((1,), (1,)), ((), ())), preferred_element_type=jnp.float32
    )
    whole_state = piece_rows
    product, whole_state = (product, whole_state)
    for turn in range(MAXR):
        active = jnp.repeat(turn >= MAXR - slot_counts, seq_length)[:, None]
        if turn > 0:
            product = lax.dot_general(
                whole_state,
                core_weight,
                (((1,), (1,)), ((), ())),
                preferred_element_type=jnp.float32,
            )
        mixed = (product + injected_input).astype(jnp.bfloat16)
        mixed_float = mixed.astype(jnp.float32)
        if turn + 1 < MAXR:
            mixed_whole = lax.all_gather(mixed, "mp", axis=1, tiled=True).astype(jnp.float32)
            inverse_rms = lax.rsqrt(jnp.sum(mixed_whole * mixed_whole, axis=1) / full_width + EPS)
            renewed = (norm_gain * mixed_whole * inverse_rms[:, None]).astype(jnp.bfloat16)
            saved.append((whole_state, mixed_float, inverse_rms, active))
            whole_state = jnp.where(active, renewed, whole_state)
        else:
            inverse_rms = lax.rsqrt(
                feature_sum(jnp.sum(mixed_float * mixed_float, axis=1)) / full_width + EPS
            )
            saved.append((whole_state, mixed_float, inverse_rms, active))
    upstream = state_cotangent.reshape(row_count, local_width).astype(jnp.float32)
    weight_grad = jnp.zeros((local_width, full_width), jnp.float32)
    for back_index in range(BP):
        whole_state, mixed_float, inverse_rms, active = saved[MAXR - 1 - back_index]
        scaled = upstream * gain_local
        inner = feature_sum(jnp.sum(scaled * mixed_float, axis=1))
        delta = (
            inverse_rms[:, None] * scaled
            - mixed_float * (inverse_rms**3 * inner / full_width)[:, None]
        )
        delta_b = jnp.where(active, delta, 0.0).astype(jnp.bfloat16)
        weight_grad = weight_grad + lax.dot_general(
            delta_b, whole_state, (((0,), (0,)), ((), ())), preferred_element_type=jnp.float32
        )
        if back_index + 1 < BP:
            partial_rows = jnp.dot(delta_b, core_weight, preferred_element_type=jnp.float32)
            summed_rows = lax.psum_scatter(
                partial_rows.astype(jnp.bfloat16), "mp", scatter_dimension=1, tiled=True
            ).astype(jnp.float32)
            upstream = jnp.where(active, summed_rows, upstream)
    return lax.psum_scatter(
        weight_grad.astype(jnp.bfloat16), "dp", scatter_dimension=1, tiled=True
    ).astype(jnp.float32)


def core_kernel(
    n_dp, n_mp, streams, full_width, cap,
    counts_in, groups_in, prelude_ref, noise_ref, cot_ref, gain_in, w_hbm,
    ds, xs,
    w_ref, w8, u0, u1, u2, y0, y1, gain_ref, counts_ref, pick_ref, inject, acc, square, scale, rms,
    cot_rows, scaled, y_last, delta_b, spread_own, total_ref, noise_rows,
    pre_all, noise_all, cot_all, red, pair_send, pair_recv, line_send, line_recv,
    w_sem, in_send, in_recv, g_send, g_recv, x_send, x_recv, own_sem, d_send, d_recv,
    red_send, red_recv, p_send, p_recv, l_send, l_recv,
):
    dp = lax.axis_index("dp")
    mp = lax.axis_index("mp")
    n_line = n_mp // 2
    line, side = mp // 2, lax.rem(mp, 2)
    blocks = n_mp // n_dp
    seq_dev, tokens, width = prelude_ref.shape
    rows = seq_dev * tokens
    part_rows = rows // streams

    w_copy = pltpu.make_async_copy(w_hbm, w_ref, w_sem)
    w_copy.start()

    barrier = pltpu.get_barrier_semaphore()
    for o in range(1, n_mp):
        pl.semaphore_signal(
            barrier, inc=1, device_id=(dp, lax.rem(mp + o, n_mp)), device_id_type=MESH
        )
    for o in range(1, n_dp):
        pl.semaphore_signal(
            barrier, inc=1, device_id=(lax.rem(dp + o, n_dp), mp), device_id_type=MESH
        )

    seqs = groups_in.shape[0]
    one, zero = jnp.int32(1), jnp.int32(0)
    group = [groups_in[i] for i in range(seqs)]
    rank = []
    for i in range(seqs):
        r = zero
        for j in range(i):
            r = r + jnp.where(group[j] == group[i], one, zero)
        rank.append(r)
    full = []
    for g in range(n_dp):
        size = zero
        for i in range(seqs):
            size = size + jnp.where(group[i] == g, one, zero)
        full.append(jnp.where(size == cap, one, zero))
    order = []
    for g in range(n_dp):
        r = zero
        for e in range(g):
            r = r + jnp.where(full[e] == full[g], one, zero)
        order.append(r)
    mine_full, mine_order = zero, zero
    for g in range(n_dp):
        mine_full = jnp.where(dp == g, full[g], mine_full)
        mine_order = jnp.where(dp == g, order[g], mine_order)
    partner = zero
    part_weight = []
    for g in range(n_dp):
        hit = full[g] * (one - mine_full) * jnp.where(order[g] == mine_order, one, zero)
        partner = partner + hit * g
        part_weight.append(hit.astype(F32))
    own_weight = mine_full.astype(F32)
    for b in range(seq_dev):
        want_group, want_rank = dp, jnp.int32(b)
        if b == seq_dev - 1:
            want_group = jnp.where(mine_full == one, dp, partner)
            want_rank = jnp.where(mine_full == one, want_rank, cap - 1)
        count = zero
        for i in range(seqs):
            hit = jnp.where(group[i] == want_group, one, zero) * jnp.where(
                rank[i] == want_rank, one, zero
            )
            count = count + hit * counts_in[i]
            pick_ref[b * seqs + i] = hit.astype(F32)
        counts_ref[pl.ds(b * tokens, tokens)] = jnp.zeros((tokens, 1), F32) + count.astype(F32)

    pl.semaphore_wait(barrier, n_mp + n_dp - 2)

    def remote(src, dst, send, recv, device):
        return pltpu.make_async_remote_copy(
            src_ref=src, dst_ref=dst, send_sem=send, recv_sem=recv,
            device_id=device, device_id_type=MESH,
        )

    in_copies = []

    def cross(which, src, dst):
        copies = []
        for o in range(1, n_dp):
            copy = remote(
                src, dst.at[dp], in_send.at[which, o], in_recv.at[which, o],
                (lax.rem(dp + o, n_dp), mp),
            )
            copy.start()
            copies.append(copy)
        in_copies.append(copies)

    cross(0, noise_ref.at[seq_dev], noise_all)
    peer = (dp, line * 2 + 1 - side)

    def gather_start(turn, s, buf):
        own = buf.at[s, mp]
        remote(own, own, g_send.at[turn, s, 1], g_recv.at[turn, s, 1], peer).start()
        for h in range(1, n_line):
            to = (dp, lax.rem(line + h, n_line) * 2 + side)
            remote(own, own, g_send.at[turn, s, 1 + h], g_recv.at[turn, s, 1 + h], to).start()

    def gather_wait(turn, s, buf, at, owner):
        remote(
            buf.at[s, owner], buf.at[s, owner], g_send.at[turn, s, at], g_recv.at[turn, s, at], peer
        ).wait_recv()

    def gather_forward(turn, s, buf, h):
        owner = lax.rem(line + n_line - h, n_line) * 2 + side
        gather_wait(turn, s, buf, 1 + h, owner)
        at = n_line + h
        remote(
            buf.at[s, owner], buf.at[s, owner], g_send.at[turn, s, at], g_recv.at[turn, s, at], peer
        ).start()

    def gather_steps(turn, s, buf, use, forwarded=False):
        def step(at, carry):
            h = jnp.where(at < 2, 0, jnp.where(at <= n_line, at - 1, at - n_line))
            other = jnp.where(at < 2, at, jnp.where(at <= n_line, 0, 1))
            owner = lax.rem(line + n_line - h, n_line) * 2 + lax.rem(side + other, 2)

            @pl.when((at == 1) | (at > n_line))
            def _():
                gather_wait(turn, s, buf, at, owner)

            if not forwarded:

                @pl.when((at >= 2) & (at <= n_line))
                def _():
                    gather_forward(turn, s, buf, h)

            use(owner)
            return carry

        lax.fori_loop(0, n_mp, step, 0)

    def each_stream(body):
        def step(s, carry):
            body(s)
            return carry

        lax.fori_loop(0, streams, step, 0)

    def third_rows(own, gathered):
        total = own_weight * own[seq_dev - 1].astype(F32)
        for q in range(n_dp):
            total = total + part_weight[q] * gathered[q].astype(F32)
        return total

    kept = (seq_dev - 1) * tokens
    for b in range(seq_dev - 1):
        noise_rows[pl.ds(b * tokens, tokens)] = noise_ref[b]
    ready = kept // part_rows

    def first_start(s):
        u0[s, mp] = noise_rows[pl.ds(s * part_rows, part_rows)]
        gather_start(0, s, u0)

    for s in range(ready):
        first_start(s)
    noise_all[dp] = noise_ref[seq_dev]
    for copy in in_copies[0]:
        copy.wait_recv()
    noise_rows[pl.ds(kept, tokens)] = third_rows(noise_ref, noise_all).astype(BF16)
    for s in range(ready, streams):
        first_start(s)
    cross(1, prelude_ref, pre_all)
    cross(2, cot_ref.at[seq_dev], cot_all)
    pre_all[dp] = prelude_ref[...]
    cot_all[dp] = cot_ref[seq_dev]

    w_copy.wait()
    waiting = [(s, h) for s in range(streams) for h in range(1, n_line)]
    for k in range(n_mp):
        w8[k] = w_ref[:, k * width : (k + 1) * width]
        gain_ref[k] = gain_in[pl.ds(k * width, width)].reshape(1, width)
        take = -(-len(waiting) // (n_mp - k))
        for s, h in waiting[:take]:
            gather_forward(0, s, u0, h)
        waiting = waiting[take:]

    for copy in in_copies[1]:
        copy.wait_recv()
    for b in range(seq_dev):

        def add(q, t, b=b):
            for i in range(seq_dev):
                t = t + pick_ref[b * seqs + q * seq_dev + i] * pre_all[q, i].astype(F32)
            return t

        inject[pl.ds(b * tokens, tokens)] = lax.fori_loop(
            0, n_dp, add, jnp.zeros((tokens, width), F32)
        )

    def rows_of(s):
        return pl.ds(pl.multiple_of(s * part_rows, part_rows), part_rows)

    def active(turn, s):
        return counts_ref[rows_of(s)] >= float(MAXR - turn)

    def first(s):
        acc[s] = jnp.zeros((part_rows, width), F32)

        def use(k):
            acc[s] += lax.dot_general(u0[s, k], w8[k], NT, preferred_element_type=F32)

        gather_steps(0, s, u0, use, forwarded=True)
        y0[s, mp] = (acc[s] + inject[rows_of(s)]).astype(BF16)
        gather_start(1, s, y0)

    each_stream(first)

    def renew(turn, s, y_all, before, after):
        live = active(turn, s)
        acc[s] = jnp.zeros((part_rows, width), F32)
        square[...] = jnp.zeros_like(square)

        def use(k):
            y = y_all[s, k].astype(F32)
            square[...] += jnp.sum(y * y, axis=1, keepdims=True)
            new = jnp.where(live, gain_ref[k] * y, before[s, k].astype(F32)).astype(BF16)
            after[s, k] = new
            acc[s] += lax.dot_general(new, w8[k], NT, preferred_element_type=F32)
            to = k // blocks
            part = lax.rem(k, blocks)
            dst = xs.at[part, turn, s, dp]

            @pl.when(to == dp)
            def _():
                pltpu.make_async_copy(after.at[s, k], dst, own_sem.at[turn, s, part]).start()

            @pl.when(to != dp)
            def _():
                remote(
                    after.at[s, k], dst, x_send.at[turn, s, k], x_recv.at[turn, s, dp, part],
                    (to, mp),
                ).start()

        gather_steps(1 + turn, s, y_all, use)
        root = lax.rsqrt(square[...] / full_width + EPS)
        rms[turn, rows_of(s)] = root
        previous = 1.0 if turn == 0 else scale[turn - 1, rows_of(s)]
        scale[turn, rows_of(s)] = jnp.where(live, root, previous)

    def second(s):
        renew(0, s, y0, u0, u1)
        y1[s, mp] = (scale[0, rows_of(s)] * acc[s] + inject[rows_of(s)]).astype(BF16)
        gather_start(2, s, y1)

    each_stream(second)

    for copy in in_copies[2]:
        copy.wait_recv()
    gain = gain_ref[mp]
    cot_rows[pl.ds(kept, tokens)] = third_rows(cot_ref, cot_all)
    for b in range(seq_dev - 1):
        cot_rows[pl.ds(b * tokens, tokens)] = cot_ref[b].astype(F32)
    scaled[...] = cot_rows[...] * gain

    def sums_start(which, s, values):
        ones = jnp.ones((4, width), F32)
        lines = [
            lax.dot_general(
                ones, v, NT, preferred_element_type=F32, precision=lax.Precision.HIGHEST
            )
            for v in values
        ]
        red[which, s, mp] = jnp.concatenate(lines * (2 // len(lines)), axis=0)
        own = red.at[which, s, mp]
        for o in range(1, n_mp):
            remote(
                own, own, red_send.at[which, s, o], red_recv.at[which, s, o],
                (dp, lax.rem(mp + o, n_mp)),
            ).start()

    def sums_end(which, s):
        own = red.at[which, s, mp]
        for o in range(1, n_mp):
            remote(
                own, own, red_send.at[which, s, o], red_recv.at[which, s, o], peer
            ).wait_recv()
        total = red[which, s, 0]
        for k in range(1, n_mp):
            total = total + red[which, s, k]
        columns = jnp.transpose(total)
        return columns[:, 0:1], columns[:, 4:5]

    def third(s):
        renew(1, s, y1, u1, u2)
        y = (scale[1, rows_of(s)] * acc[s] + inject[rows_of(s)]).astype(BF16).astype(F32)
        y_last[rows_of(s)] = y
        sums_start(0, s, (y * y, scaled[rows_of(s)] * y))

    each_stream(third)

    dp_pair, dp_side = dp // 2, lax.rem(dp, 2)
    n_pair = n_dp // 2
    dp_peer = (dp_pair * 2 + 1 - dp_side, mp)

    def spread_copies(which, s):
        own, dst = spread_own.at[which, s], ds.at[which, s, dp]
        copies = []
        for h in range(1, n_pair):
            to = (lax.rem(dp_pair + h, n_pair) * 2 + dp_side, mp)
            copies.append(remote(own, dst, d_send.at[which, s, h], d_recv.at[which, s, h], to))
        copies.append(remote(own, dst, d_send.at[which, s, 0], d_recv.at[which, s, 0], dp_peer))
        return copies, pltpu.make_async_copy(own, dst, own_sem.at[which, s, blocks])

    def spread_start(which, s, values):
        spread_own[which, s] = values
        copies, local_copy = spread_copies(which, s)
        for copy in copies:
            copy.start()
        local_copy.start()

    def spread_forwards(which, s):
        forwards = []
        for h in range(1, n_pair):
            held = ds.at[which, s, lax.rem(dp_pair + n_pair - h, n_pair) * 2 + dp_side]
            f = n_pair + h
            forwards.append(
                remote(held, held, d_send.at[which, s, f], d_recv.at[which, s, f], dp_peer)
            )
        return forwards

    def spread_forward(which, s):
        copies, unused = spread_copies(which, s)
        for copy, forward in zip(copies, spread_forwards(which, s)):
            copy.wait_recv()
            forward.start()

    def pair_copy(s, at):
        return remote(
            pair_send.at[s, at], pair_recv.at[s, at], p_send.at[s, at], p_recv.at[s, at], peer
        )

    def line_copy(s, at):
        to = (dp, lax.rem(line + at + 1, n_line) * 2 + side)
        return remote(
            line_send.at[s, at], line_recv.at[s, at], l_send.at[s, at], l_recv.at[s, at], to
        )

    def back_first(s):
        square2, inner2 = sums_end(0, s)
        root = lax.rsqrt(square2 / full_width + EPS)
        y = y_last[rows_of(s)]
        delta = jnp.where(
            active(2, s),
            root * scaled[rows_of(s)] - y * (root * root * root * inner2 / full_width),
            0.0,
        )
        delta_b[s] = delta.astype(BF16)

        def pair_step(at, carry):
            to_line = lax.rem(line + at + 1, n_line)
            product = jnp.dot(
                delta_b[s], w8[to_line * 2 + 1 - side], preferred_element_type=F32
            )
            pair_send[s, at] = product.astype(BF16)
            pair_copy(s, at).start()
            return carry

        lax.fori_loop(0, n_line, pair_step, 0)
        spread_start(1, s, (delta * scale[1, rows_of(s)]).astype(BF16))
        inner = delta_b[s].astype(F32) * acc[s]
        sums_start(1, s, (inner,))

    each_stream(back_first)

    def back_second(s):
        def line_step(at, carry):
            to_line = lax.rem(line + at + 1, n_line)
            product = jnp.dot(delta_b[s], w8[to_line * 2 + side], preferred_element_type=F32)
            pair_copy(s, at).wait_recv()
            total = product.astype(BF16).astype(F32) + pair_recv[s, at].astype(F32)
            total_ref[s] = total

            @pl.when(at < n_line - 1)
            def _():
                line_send[s, at] = total.astype(BF16)
                line_copy(s, at).start()

            return carry

        lax.fori_loop(0, n_line, line_step, 0)

    each_stream(back_second)
    for s in range(streams):
        spread_forward(1, s)

    def back_third(s):
        unused, inner = sums_end(1, s)
        total = total_ref[s]
        for at in range(n_line - 1):
            line_copy(s, at).wait_recv()
            total = total + line_recv[s, at].astype(F32)
        upstream = jnp.where(active(2, s), total, cot_rows[rows_of(s)])
        y = y1[s, mp].astype(F32)
        root = rms[1, rows_of(s)]
        delta = jnp.where(
            active(1, s),
            root * (upstream * gain) - y * (root * root * root * inner / full_width),
            0.0,
        )
        spread_start(0, s, (delta * scale[0, rows_of(s)]).astype(BF16))

    each_stream(back_third)
    for s in range(streams):
        spread_forward(0, s)

    def finish(s):
        for which in range(BP):
            copies, local_copy = spread_copies(which, s)
            copies[-1].wait_recv()
            for copy in spread_forwards(which, s):
                copy.wait()
            for copy in copies:
                copy.wait_send()
            local_copy.wait()
            for part in range(blocks):
                pltpu.make_async_copy(
                    u1.at[s, 0], xs.at[part, which, s, dp], own_sem.at[which, s, part]
                ).wait()
                for h in range(1, n_dp):
                    q = lax.rem(dp + h, n_dp)
                    copy = remote(
                        u1.at[s, 0], xs.at[part, which, s, q],
                        x_send.at[which, s, q * blocks + part], x_recv.at[which, s, q, part],
                        (q, mp),
                    )
                    copy.wait()
            own = red.at[which, s, mp]
            for o in range(1, n_mp):
                remote(
                    own, own, red_send.at[which, s, o], red_recv.at[which, s, o], peer
                ).wait_send()
        for turn, buf in enumerate((u0, y0, y1)):
            for at in range(1, n_mp):
                remote(
                    buf.at[s, mp], buf.at[s, mp], g_send.at[turn, s, at], g_recv.at[turn, s, at],
                    peer,
                ).wait_send()
        for at in range(n_line):
            pair_copy(s, at).wait_send()
        for at in range(n_line - 1):
            line_copy(s, at).wait_send()

    each_stream(finish)
    for copies in in_copies:
        for copy in copies:
            copy.wait_send()


def grad_kernel(ds_ref, xs_ref, out_ref):
    width = ds_ref.shape[-1]
    left = ds_ref[...].reshape(-1, width)
    depth = left.shape[0]
    full = xs_ref.shape[-1]
    for part in range(xs_ref.shape[0]):
        right = xs_ref[part].reshape(depth, full)
        out_ref[:, part * full : (part + 1) * full] = lax.dot_general(
            left, right, TN, preferred_element_type=F32
        )


def fused(
    n_dp, n_mp, streams,
    prelude_output, init_noise, core_weight, norm_gain, state_cotangent, step_counts, group_table,
):
    width, full_width = core_weight.shape
    seq_dev, tokens = prelude_output.shape[:2]
    cap = init_noise.shape[0]
    seqs = group_table.shape[0]
    rows = seq_dev * tokens
    part_rows = rows // streams
    blocks = n_mp // n_dp
    n_line, n_pair = n_mp // 2, n_dp // 2
    vmem = pl.BlockSpec(memory_space=pltpu.VMEM)
    smem = pl.BlockSpec(memory_space=pltpu.SMEM)
    any_space = pl.BlockSpec(memory_space=pl.ANY)
    state = pltpu.VMEM((streams, n_mp, part_rows, width), BF16)
    row_f32 = pltpu.VMEM((rows, width), F32)
    stream_f32 = pltpu.VMEM((streams, part_rows, width), F32)
    pieces = pltpu.VMEM((streams, n_line, part_rows, width), BF16)
    dma = pltpu.SemaphoreType.DMA
    scratch = [
        pltpu.VMEM((width, full_width), BF16),
        pltpu.VMEM((n_mp, width, width), BF16),
        state, state, state, state, state,
        pltpu.VMEM((n_mp, 1, width), F32),
        pltpu.VMEM((rows, 1), F32),
        pltpu.SMEM((seq_dev * seqs,), F32),
        row_f32, stream_f32,
        pltpu.VMEM((part_rows, 1), F32),
        pltpu.VMEM((BP, rows, 1), F32),
        pltpu.VMEM((BP, rows, 1), F32),
        row_f32, row_f32, row_f32,
        pltpu.VMEM((streams, part_rows, width), BF16),
        pltpu.VMEM((BP, streams, part_rows, width), BF16),
        stream_f32,
        pltpu.VMEM((rows, width), BF16),
        pltpu.VMEM((n_dp, seq_dev, tokens, width), BF16),
        pltpu.VMEM((n_dp, tokens, width), BF16),
        pltpu.VMEM((n_dp, tokens, width), BF16),
        pltpu.VMEM((BP, streams, n_mp, 8, part_rows), F32),
        pieces, pieces, pieces, pieces,
        dma,
        dma((3, n_dp)), dma((3, n_dp)),
        dma((MAXR, streams, n_mp)), dma((MAXR, streams, n_mp)),
        dma((BP, streams, n_mp)), dma((BP, streams, n_dp, blocks)),
        dma((BP, streams, blocks + 1)),
        dma((BP, streams, 2 * n_pair)), dma((BP, streams, 2 * n_pair)),
        dma((BP, streams, n_mp)), dma((BP, streams, n_mp)),
        dma((streams, n_line)), dma((streams, n_line)),
        dma((streams, n_line)), dma((streams, n_line)),
    ]
    deltas, states = pl.pallas_call(
        functools.partial(core_kernel, n_dp, n_mp, streams, full_width, cap),
        out_shape=(
            jax.ShapeDtypeStruct((BP, streams, n_dp, part_rows, width), BF16),
            jax.ShapeDtypeStruct((blocks, BP, streams, n_dp, part_rows, width), BF16),
        ),
        in_specs=[smem] * 2 + [vmem] * 4 + [any_space],
        out_specs=(any_space, any_space),
        scratch_shapes=scratch,
        compiler_params=pltpu.CompilerParams(
            collective_id=0, has_side_effects=True, vmem_limit_bytes=56 * 1024 * 1024
        ),
        cost_estimate=pl.CostEstimate(
            flops=2 * rows * full_width * width * 4, bytes_accessed=20_000_000, transcendentals=0
        ),
    )(
        step_counts, group_table, prelude_output, init_noise, state_cotangent,
        norm_gain, core_weight,
    )
    tile = 256
    return pl.pallas_call(
        grad_kernel,
        grid=(pl.cdiv(width, tile),),
        out_shape=jax.ShapeDtypeStruct((width, blocks * width), F32),
        in_specs=[
            pl.BlockSpec((BP, streams, n_dp, part_rows, tile), lambda i: (0, 0, 0, 0, i)),
            pl.BlockSpec(states.shape, lambda i: (0,) * 6),
        ],
        out_specs=pl.BlockSpec((tile, blocks * width), lambda i: (i, 0)),
        compiler_params=pltpu.CompilerParams(vmem_limit_bytes=60 * 1024 * 1024),
    )(deltas, states)


def solution(mesh):
    n_dp, n_mp = mesh.shape["dp"], mesh.shape["mp"]
    paired = n_mp % n_dp == 0 and n_mp % 2 == 0 and n_dp % 2 == 0
    return jax.shard_map(
        functools.partial(fused, n_dp, n_mp, STREAMS) if paired else local,
        mesh=mesh,
        in_specs=(
            P("dp", None, "mp"),
            P("dp", None, "mp"),
            P("mp", None),
            P(),
            P("dp", None, "mp"),
            P(),
            P(),
        ),
        out_specs=P("mp", "dp"),
        check_vma=False,
    )
```

```python
import functools

import jax
import jax.numpy as jnp
from jax import lax
from jax.experimental import pallas as pl
from jax.experimental.pallas import tpu as pltpu
from jax.sharding import PartitionSpec as P

MESH = pl.DeviceIdType.MESH
NT = (((1,), (1,)), ((), ()))
TN = (((0,), (0,)), ((), ()))
STREAMS = 2
F32 = jnp.float32
BF16 = jnp.bfloat16
MAXR = 3
BP = 2


EPS = 1e-06


def local(
    prelude_output, init_noise, core_weight, norm_gain, state_cotangent, step_counts, group_table
):
    full_width = core_weight.shape[1]
    local_width = core_weight.shape[0]
    slot_total = init_noise.shape[0]
    seq_length = init_noise.shape[1]
    row_count = slot_total * seq_length
    my_group = lax.axis_index("dp")
    column_first = lax.axis_index("mp") * local_width
    seq_total = group_table.shape[0]
    seq_index = jnp.arange(seq_total, dtype=jnp.int32)
    earlier = (group_table[:, None] == group_table[None, :]) & (
        seq_index[None, :] < seq_index[:, None]
    )
    slot_rank = jnp.sum(earlier.astype(jnp.int32), axis=1)
    selected_rows = (group_table[None, :] == my_group) & (
        slot_rank[None, :] == jnp.arange(slot_total, dtype=jnp.int32)[:, None]
    )
    slot_counts = jnp.sum(jnp.where(selected_rows, step_counts[None, :], 0), axis=1)
    chosen_weights = selected_rows.astype(jnp.bfloat16)
    injected_input = jnp.einsum(
        "br,ref->bef",
        chosen_weights,
        lax.all_gather(prelude_output, "dp", axis=0, tiled=True),
        preferred_element_type=jnp.float32,
    ).reshape(row_count, local_width)
    gain_local = lax.dynamic_slice_in_dim(norm_gain, column_first, local_width, 0)

    def feature_sum(values):
        return lax.psum(values, "mp")

    shard_state = init_noise.reshape(row_count, local_width)
    saved = []
    piece_rows = lax.all_gather(shard_state, "mp", axis=1, tiled=True)
    product = lax.dot_general(
        piece_rows, core_weight, (((1,), (1,)), ((), ())), preferred_element_type=jnp.float32
    )
    whole_state = piece_rows
    product, whole_state = (product, whole_state)
    for turn in range(MAXR):
        active = jnp.repeat(turn >= MAXR - slot_counts, seq_length)[:, None]
        if turn > 0:
            product = lax.dot_general(
                whole_state,
                core_weight,
                (((1,), (1,)), ((), ())),
                preferred_element_type=jnp.float32,
            )
        mixed = (product + injected_input).astype(jnp.bfloat16)
        mixed_float = mixed.astype(jnp.float32)
        if turn + 1 < MAXR:
            mixed_whole = lax.all_gather(mixed, "mp", axis=1, tiled=True).astype(jnp.float32)
            inverse_rms = lax.rsqrt(jnp.sum(mixed_whole * mixed_whole, axis=1) / full_width + EPS)
            renewed = (norm_gain * mixed_whole * inverse_rms[:, None]).astype(jnp.bfloat16)
            saved.append((whole_state, mixed_float, inverse_rms, active))
            whole_state = jnp.where(active, renewed, whole_state)
        else:
            inverse_rms = lax.rsqrt(
                feature_sum(jnp.sum(mixed_float * mixed_float, axis=1)) / full_width + EPS
            )
            saved.append((whole_state, mixed_float, inverse_rms, active))
    upstream = state_cotangent.reshape(row_count, local_width).astype(jnp.float32)
    weight_grad = jnp.zeros((local_width, full_width), jnp.float32)
    for back_index in range(BP):
        whole_state, mixed_float, inverse_rms, active = saved[MAXR - 1 - back_index]
        scaled = upstream * gain_local
        inner = feature_sum(jnp.sum(scaled * mixed_float, axis=1))
        delta = (
            inverse_rms[:, None] * scaled
            - mixed_float * (inverse_rms**3 * inner / full_width)[:, None]
        )
        delta_b = jnp.where(active, delta, 0.0).astype(jnp.bfloat16)
        weight_grad = weight_grad + lax.dot_general(
            delta_b, whole_state, (((0,), (0,)), ((), ())), preferred_element_type=jnp.float32
        )
        if back_index + 1 < BP:
            partial_rows = jnp.dot(delta_b, core_weight, preferred_element_type=jnp.float32)
            summed_rows = lax.psum_scatter(
                partial_rows.astype(jnp.bfloat16), "mp", scatter_dimension=1, tiled=True
            ).astype(jnp.float32)
            upstream = jnp.where(active, summed_rows, upstream)
    return lax.psum_scatter(
        weight_grad.astype(jnp.bfloat16), "dp", scatter_dimension=1, tiled=True
    ).astype(jnp.float32)


def core_kernel(
    n_dp, n_mp, streams, full_width, cap,
    counts_in, groups_in, prelude_ref, noise_ref, cot_ref, gain_in, w_hbm,
    ds, xs,
    w_ref, w8, u0, u1, u2, y0, y1, gain_ref, counts_ref, pick_ref, inject, acc, square, scale, rms,
    cot_rows, scaled, y_last, delta_b, spread_own, total_ref, noise_rows,
    pre_all, noise_all, cot_all, red, pair_send, pair_recv, line_send, line_recv,
    w_sem, in_send, in_recv, g_send, g_recv, x_send, x_recv, own_sem, d_send, d_recv,
    red_send, red_recv, p_send, p_recv, l_send, l_recv,
):
    dp = lax.axis_index("dp")
    mp = lax.axis_index("mp")
    n_line = n_mp // 2
    line, side = mp // 2, lax.rem(mp, 2)
    blocks = n_mp // n_dp
    seq_dev, tokens, width = prelude_ref.shape
    rows = seq_dev * tokens
    part_rows = rows // streams

    w_copy = pltpu.make_async_copy(w_hbm, w_ref, w_sem)
    w_copy.start()

    barrier = pltpu.get_barrier_semaphore()
    for o in range(1, n_mp):
        pl.semaphore_signal(
            barrier, inc=1, device_id=(dp, lax.rem(mp + o, n_mp)), device_id_type=MESH
        )
    for o in range(1, n_dp):
        pl.semaphore_signal(
            barrier, inc=1, device_id=(lax.rem(dp + o, n_dp), mp), device_id_type=MESH
        )

    seqs = groups_in.shape[0]
    one, zero = jnp.int32(1), jnp.int32(0)
    group = [groups_in[i] for i in range(seqs)]
    rank = []
    for i in range(seqs):
        r = zero
        for j in range(i):
            r = r + jnp.where(group[j] == group[i], one, zero)
        rank.append(r)
    full = []
    for g in range(n_dp):
        size = zero
        for i in range(seqs):
            size = size + jnp.where(group[i] == g, one, zero)
        full.append(jnp.where(size == cap, one, zero))
    order = []
    for g in range(n_dp):
        r = zero
        for e in range(g):
            r = r + jnp.where(full[e] == full[g], one, zero)
        order.append(r)
    mine_full, mine_order = zero, zero
    for g in range(n_dp):
        mine_full = jnp.where(dp == g, full[g], mine_full)
        mine_order = jnp.where(dp == g, order[g], mine_order)
    partner = zero
    part_weight = []
    for g in range(n_dp):
        hit = full[g] * (one - mine_full) * jnp.where(order[g] == mine_order, one, zero)
        partner = partner + hit * g
        part_weight.append(hit.astype(F32))
    own_weight = mine_full.astype(F32)
    for b in range(seq_dev):
        want_group, want_rank = dp, jnp.int32(b)
        if b == seq_dev - 1:
            want_group = jnp.where(mine_full == one, dp, partner)
            want_rank = jnp.where(mine_full == one, want_rank, cap - 1)
        count = zero
        for i in range(seqs):
            hit = jnp.where(group[i] == want_group, one, zero) * jnp.where(
                rank[i] == want_rank, one, zero
            )
            count = count + hit * counts_in[i]
            pick_ref[b * seqs + i] = hit.astype(F32)
        counts_ref[pl.ds(b * tokens, tokens)] = jnp.zeros((tokens, 1), F32) + count.astype(F32)

    pl.semaphore_wait(barrier, n_mp + n_dp - 2)

    def remote(src, dst, send, recv, device):
        return pltpu.make_async_remote_copy(
            src_ref=src, dst_ref=dst, send_sem=send, recv_sem=recv,
            device_id=device, device_id_type=MESH,
        )

    in_copies = []

    def cross(which, src, dst):
        copies = []
        for o in range(1, n_dp):
            copy = remote(
                src, dst.at[dp], in_send.at[which, o], in_recv.at[which, o],
                (lax.rem(dp + o, n_dp), mp),
            )
            copy.start()
            copies.append(copy)
        in_copies.append(copies)

    cross(0, noise_ref.at[seq_dev], noise_all)
    peer = (dp, line * 2 + 1 - side)

    def gather_start(turn, s, buf):
        own = buf.at[s, mp]
        remote(own, own, g_send.at[turn, s, 1], g_recv.at[turn, s, 1], peer).start()
        for h in range(1, n_line):
            to = (dp, lax.rem(line + h, n_line) * 2 + side)
            remote(own, own, g_send.at[turn, s, 1 + h], g_recv.at[turn, s, 1 + h], to).start()

    def gather_wait(turn, s, buf, at, owner):
        remote(
            buf.at[s, owner], buf.at[s, owner], g_send.at[turn, s, at], g_recv.at[turn, s, at], peer
        ).wait_recv()

    def gather_forward(turn, s, buf, h):
        owner = lax.rem(line + n_line - h, n_line) * 2 + side
        gather_wait(turn, s, buf, 1 + h, owner)
        at = n_line + h
        remote(
            buf.at[s, owner], buf.at[s, owner], g_send.at[turn, s, at], g_recv.at[turn, s, at], peer
        ).start()

    def gather_steps(turn, s, buf, use, forwarded=False):
        def step(at, carry):
            h = jnp.where(at < 2, 0, jnp.where(at <= n_line, at - 1, at - n_line))
            other = jnp.where(at < 2, at, jnp.where(at <= n_line, 0, 1))
            owner = lax.rem(line + n_line - h, n_line) * 2 + lax.rem(side + other, 2)

            @pl.when((at == 1) | (at > n_line))
            def _():
                gather_wait(turn, s, buf, at, owner)

            if not forwarded:

                @pl.when((at >= 2) & (at <= n_line))
                def _():
                    gather_forward(turn, s, buf, h)

            use(owner)
            return carry

        lax.fori_loop(0, n_mp, step, 0)

    def each_stream(body):
        def step(s, carry):
            body(s)
            return carry

        lax.fori_loop(0, streams, step, 0)

    def third_rows(own, gathered):
        total = own_weight * own[seq_dev - 1].astype(F32)
        for q in range(n_dp):
            total = total + part_weight[q] * gathered[q].astype(F32)
        return total

    kept = (seq_dev - 1) * tokens
    for b in range(seq_dev - 1):
        noise_rows[pl.ds(b * tokens, tokens)] = noise_ref[b]

    def first_start(s):
        u0[s, mp] = noise_rows[pl.ds(s * part_rows, part_rows)]
        gather_start(0, s, u0)

    first_start(0)
    noise_all[dp] = noise_ref[seq_dev]
    for copy in in_copies[0]:
        copy.wait_recv()
    noise_rows[pl.ds(kept, tokens)] = third_rows(noise_ref, noise_all).astype(BF16)
    cross(1, prelude_ref, pre_all)
    cross(2, cot_ref.at[seq_dev], cot_all)
    pre_all[dp] = prelude_ref[...]
    cot_all[dp] = cot_ref[seq_dev]

    w_copy.wait()
    waiting = list(range(1, n_line))
    for k in range(n_mp):
        w8[k] = w_ref[:, k * width : (k + 1) * width]
        gain_ref[k] = gain_in[pl.ds(k * width, width)].reshape(1, width)
        if k >= 1 and waiting:
            gather_forward(0, 0, u0, waiting.pop(0))
            if not waiting:
                for s in range(1, streams):
                    first_start(s)

    for copy in in_copies[1]:
        copy.wait_recv()
    for b in range(seq_dev):

        def add(q, t, b=b):
            for i in range(seq_dev):
                t = t + pick_ref[b * seqs + q * seq_dev + i] * pre_all[q, i].astype(F32)
            return t

        inject[pl.ds(b * tokens, tokens)] = lax.fori_loop(
            0, n_dp, add, jnp.zeros((tokens, width), F32)
        )

    def rows_of(s):
        return pl.ds(pl.multiple_of(s * part_rows, part_rows), part_rows)

    def active(turn, s):
        return counts_ref[rows_of(s)] >= float(MAXR - turn)

    def first(s, forwarded):
        acc[s] = jnp.zeros((part_rows, width), F32)

        def use(k):
            acc[s] += lax.dot_general(u0[s, k], w8[k], NT, preferred_element_type=F32)

        gather_steps(0, s, u0, use, forwarded=forwarded)
        y0[s, mp] = (acc[s] + inject[rows_of(s)]).astype(BF16)
        gather_start(1, s, y0)

    for s in range(streams):
        first(s, s == 0)

    def renew(turn, s, y_all, before, after):
        live = active(turn, s)
        acc[s] = jnp.zeros((part_rows, width), F32)
        square[...] = jnp.zeros_like(square)

        def use(k):
            y = y_all[s, k].astype(F32)
            square[...] += jnp.sum(y * y, axis=1, keepdims=True)
            new = jnp.where(live, gain_ref[k] * y, before[s, k].astype(F32)).astype(BF16)
            after[s, k] = new
            acc[s] += lax.dot_general(new, w8[k], NT, preferred_element_type=F32)
            to = k // blocks
            part = lax.rem(k, blocks)
            dst = xs.at[part, turn, s, dp]

            @pl.when(to == dp)
            def _():
                pltpu.make_async_copy(after.at[s, k], dst, own_sem.at[turn, s, part]).start()

            @pl.when(to != dp)
            def _():
                remote(
                    after.at[s, k], dst, x_send.at[turn, s, k], x_recv.at[turn, s, dp, part],
                    (to, mp),
                ).start()

        gather_steps(1 + turn, s, y_all, use)
        root = lax.rsqrt(square[...] / full_width + EPS)
        rms[turn, rows_of(s)] = root
        previous = 1.0 if turn == 0 else scale[turn - 1, rows_of(s)]
        scale[turn, rows_of(s)] = jnp.where(live, root, previous)

    def second(s):
        renew(0, s, y0, u0, u1)
        y1[s, mp] = (scale[0, rows_of(s)] * acc[s] + inject[rows_of(s)]).astype(BF16)
        gather_start(2, s, y1)

    each_stream(second)

    for copy in in_copies[2]:
        copy.wait_recv()
    gain = gain_ref[mp]
    cot_rows[pl.ds(kept, tokens)] = third_rows(cot_ref, cot_all)
    for b in range(seq_dev - 1):
        cot_rows[pl.ds(b * tokens, tokens)] = cot_ref[b].astype(F32)
    scaled[...] = cot_rows[...] * gain

    def sums_start(which, s, values):
        ones = jnp.ones((4, width), F32)
        lines = [
            lax.dot_general(
                ones, v, NT, preferred_element_type=F32, precision=lax.Precision.HIGHEST
            )
            for v in values
        ]
        red[which, s, mp] = jnp.concatenate(lines * (2 // len(lines)), axis=0)
        own = red.at[which, s, mp]
        for o in range(1, n_mp):
            remote(
                own, own, red_send.at[which, s, o], red_recv.at[which, s, o],
                (dp, lax.rem(mp + o, n_mp)),
            ).start()

    def sums_end(which, s):
        own = red.at[which, s, mp]
        for o in range(1, n_mp):
            remote(
                own, own, red_send.at[which, s, o], red_recv.at[which, s, o], peer
            ).wait_recv()
        total = red[which, s, 0]
        for k in range(1, n_mp):
            total = total + red[which, s, k]
        columns = jnp.transpose(total)
        return columns[:, 0:1], columns[:, 4:5]

    def third(s):
        renew(1, s, y1, u1, u2)
        y = (scale[1, rows_of(s)] * acc[s] + inject[rows_of(s)]).astype(BF16).astype(F32)
        y_last[rows_of(s)] = y
        sums_start(0, s, (y * y, scaled[rows_of(s)] * y))

    each_stream(third)

    dp_pair, dp_side = dp // 2, lax.rem(dp, 2)
    n_pair = n_dp // 2
    dp_peer = (dp_pair * 2 + 1 - dp_side, mp)

    def spread_copies(which, s):
        own, dst = spread_own.at[which, s], ds.at[which, s, dp]
        copies = []
        for h in range(1, n_pair):
            to = (lax.rem(dp_pair + h, n_pair) * 2 + dp_side, mp)
            copies.append(remote(own, dst, d_send.at[which, s, h], d_recv.at[which, s, h], to))
        copies.append(remote(own, dst, d_send.at[which, s, 0], d_recv.at[which, s, 0], dp_peer))
        return copies, pltpu.make_async_copy(own, dst, own_sem.at[which, s, blocks])

    def spread_start(which, s, values):
        spread_own[which, s] = values
        copies, local_copy = spread_copies(which, s)
        for copy in copies:
            copy.start()
        local_copy.start()

    def spread_forwards(which, s):
        forwards = []
        for h in range(1, n_pair):
            held = ds.at[which, s, lax.rem(dp_pair + n_pair - h, n_pair) * 2 + dp_side]
            f = n_pair + h
            forwards.append(
                remote(held, held, d_send.at[which, s, f], d_recv.at[which, s, f], dp_peer)
            )
        return forwards

    def spread_forward(which, s):
        copies, unused = spread_copies(which, s)
        for copy, forward in zip(copies, spread_forwards(which, s)):
            copy.wait_recv()
            forward.start()

    def pair_copy(s, at):
        return remote(
            pair_send.at[s, at], pair_recv.at[s, at], p_send.at[s, at], p_recv.at[s, at], peer
        )

    def line_copy(s, at):
        to = (dp, lax.rem(line + at + 1, n_line) * 2 + side)
        return remote(
            line_send.at[s, at], line_recv.at[s, at], l_send.at[s, at], l_recv.at[s, at], to
        )

    def back_first(s):
        square2, inner2 = sums_end(0, s)
        root = lax.rsqrt(square2 / full_width + EPS)
        y = y_last[rows_of(s)]
        delta = jnp.where(
            active(2, s),
            root * scaled[rows_of(s)] - y * (root * root * root * inner2 / full_width),
            0.0,
        )
        delta_b[s] = delta.astype(BF16)

        def pair_step(at, carry):
            to_line = lax.rem(line + at + 1, n_line)
            product = jnp.dot(
                delta_b[s], w8[to_line * 2 + 1 - side], preferred_element_type=F32
            )
            pair_send[s, at] = product.astype(BF16)
            pair_copy(s, at).start()
            return carry

        lax.fori_loop(0, n_line, pair_step, 0)
        spread_start(1, s, (delta * scale[1, rows_of(s)]).astype(BF16))
        inner = delta_b[s].astype(F32) * acc[s]
        sums_start(1, s, (inner,))

    each_stream(back_first)

    def back_second(s):
        def line_step(at, carry):
            to_line = lax.rem(line + at + 1, n_line)
            product = jnp.dot(delta_b[s], w8[to_line * 2 + side], preferred_element_type=F32)
            pair_copy(s, at).wait_recv()
            total = product.astype(BF16).astype(F32) + pair_recv[s, at].astype(F32)
            total_ref[s] = total

            @pl.when(at < n_line - 1)
            def _():
                line_send[s, at] = total.astype(BF16)
                line_copy(s, at).start()

            return carry

        lax.fori_loop(0, n_line, line_step, 0)

    each_stream(back_second)
    for s in range(streams):
        spread_forward(1, s)

    def back_third(s):
        unused, inner = sums_end(1, s)
        total = total_ref[s]
        for at in range(n_line - 1):
            line_copy(s, at).wait_recv()
            total = total + line_recv[s, at].astype(F32)
        upstream = jnp.where(active(2, s), total, cot_rows[rows_of(s)])
        y = y1[s, mp].astype(F32)
        root = rms[1, rows_of(s)]
        delta = jnp.where(
            active(1, s),
            root * (upstream * gain) - y * (root * root * root * inner / full_width),
            0.0,
        )
        spread_start(0, s, (delta * scale[0, rows_of(s)]).astype(BF16))

    each_stream(back_third)
    for s in range(streams):
        spread_forward(0, s)

    def finish(s):
        for which in range(BP):
            copies, local_copy = spread_copies(which, s)
            copies[-1].wait_recv()
            for copy in spread_forwards(which, s):
                copy.wait()
            for copy in copies:
                copy.wait_send()
            local_copy.wait()
            for part in range(blocks):
                pltpu.make_async_copy(
                    u1.at[s, 0], xs.at[part, which, s, dp], own_sem.at[which, s, part]
                ).wait()
                for h in range(1, n_dp):
                    q = lax.rem(dp + h, n_dp)
                    copy = remote(
                        u1.at[s, 0], xs.at[part, which, s, q],
                        x_send.at[which, s, q * blocks + part], x_recv.at[which, s, q, part],
                        (q, mp),
                    )
                    copy.wait()
            own = red.at[which, s, mp]
            for o in range(1, n_mp):
                remote(
                    own, own, red_send.at[which, s, o], red_recv.at[which, s, o], peer
                ).wait_send()
        for turn, buf in enumerate((u0, y0, y1)):
            for at in range(1, n_mp):
                remote(
                    buf.at[s, mp], buf.at[s, mp], g_send.at[turn, s, at], g_recv.at[turn, s, at],
                    peer,
                ).wait_send()
        for at in range(n_line):
            pair_copy(s, at).wait_send()
        for at in range(n_line - 1):
            line_copy(s, at).wait_send()

    each_stream(finish)
    for copies in in_copies:
        for copy in copies:
            copy.wait_send()


def grad_kernel(ds_ref, xs_ref, out_ref):
    width = ds_ref.shape[-1]
    left = ds_ref[...].reshape(-1, width)
    depth = left.shape[0]
    full = xs_ref.shape[-1]
    for part in range(xs_ref.shape[0]):
        right = xs_ref[part].reshape(depth, full)
        out_ref[:, part * full : (part + 1) * full] = lax.dot_general(
            left, right, TN, preferred_element_type=F32
        )


def fused(
    n_dp, n_mp, streams,
    prelude_output, init_noise, core_weight, norm_gain, state_cotangent, step_counts, group_table,
):
    width, full_width = core_weight.shape
    seq_dev, tokens = prelude_output.shape[:2]
    cap = init_noise.shape[0]
    seqs = group_table.shape[0]
    rows = seq_dev * tokens
    part_rows = rows // streams
    blocks = n_mp // n_dp
    n_line, n_pair = n_mp // 2, n_dp // 2
    vmem = pl.BlockSpec(memory_space=pltpu.VMEM)
    smem = pl.BlockSpec(memory_space=pltpu.SMEM)
    any_space = pl.BlockSpec(memory_space=pl.ANY)
    state = pltpu.VMEM((streams, n_mp, part_rows, width), BF16)
    row_f32 = pltpu.VMEM((rows, width), F32)
    stream_f32 = pltpu.VMEM((streams, part_rows, width), F32)
    pieces = pltpu.VMEM((streams, n_line, part_rows, width), BF16)
    dma = pltpu.SemaphoreType.DMA
    scratch = [
        pltpu.VMEM((width, full_width), BF16),
        pltpu.VMEM((n_mp, width, width), BF16),
        state, state, state, state, state,
        pltpu.VMEM((n_mp, 1, width), F32),
        pltpu.VMEM((rows, 1), F32),
        pltpu.SMEM((seq_dev * seqs,), F32),
        row_f32, stream_f32,
        pltpu.VMEM((part_rows, 1), F32),
        pltpu.VMEM((BP, rows, 1), F32),
        pltpu.VMEM((BP, rows, 1), F32),
        row_f32, row_f32, row_f32,
        pltpu.VMEM((streams, part_rows, width), BF16),
        pltpu.VMEM((BP, streams, part_rows, width), BF16),
        stream_f32,
        pltpu.VMEM((rows, width), BF16),
        pltpu.VMEM((n_dp, seq_dev, tokens, width), BF16),
        pltpu.VMEM((n_dp, tokens, width), BF16),
        pltpu.VMEM((n_dp, tokens, width), BF16),
        pltpu.VMEM((BP, streams, n_mp, 8, part_rows), F32),
        pieces, pieces, pieces, pieces,
        dma,
        dma((3, n_dp)), dma((3, n_dp)),
        dma((MAXR, streams, n_mp)), dma((MAXR, streams, n_mp)),
        dma((BP, streams, n_mp)), dma((BP, streams, n_dp, blocks)),
        dma((BP, streams, blocks + 1)),
        dma((BP, streams, 2 * n_pair)), dma((BP, streams, 2 * n_pair)),
        dma((BP, streams, n_mp)), dma((BP, streams, n_mp)),
        dma((streams, n_line)), dma((streams, n_line)),
        dma((streams, n_line)), dma((streams, n_line)),
    ]
    deltas, states = pl.pallas_call(
        functools.partial(core_kernel, n_dp, n_mp, streams, full_width, cap),
        out_shape=(
            jax.ShapeDtypeStruct((BP, streams, n_dp, part_rows, width), BF16),
            jax.ShapeDtypeStruct((blocks, BP, streams, n_dp, part_rows, width), BF16),
        ),
        in_specs=[smem] * 2 + [vmem] * 4 + [any_space],
        out_specs=(any_space, any_space),
        scratch_shapes=scratch,
        compiler_params=pltpu.CompilerParams(
            collective_id=0, has_side_effects=True, vmem_limit_bytes=56 * 1024 * 1024
        ),
        cost_estimate=pl.CostEstimate(
            flops=2 * rows * full_width * width * 4, bytes_accessed=20_000_000, transcendentals=0
        ),
    )(
        step_counts, group_table, prelude_output, init_noise, state_cotangent,
        norm_gain, core_weight,
    )
    tile = 256
    return pl.pallas_call(
        grad_kernel,
        grid=(pl.cdiv(width, tile),),
        out_shape=jax.ShapeDtypeStruct((width, blocks * width), F32),
        in_specs=[
            pl.BlockSpec((BP, streams, n_dp, part_rows, tile), lambda i: (0, 0, 0, 0, i)),
            pl.BlockSpec(states.shape, lambda i: (0,) * 6),
        ],
        out_specs=pl.BlockSpec((tile, blocks * width), lambda i: (i, 0)),
        compiler_params=pltpu.CompilerParams(vmem_limit_bytes=60 * 1024 * 1024),
    )(deltas, states)


def solution(mesh):
    n_dp, n_mp = mesh.shape["dp"], mesh.shape["mp"]
    paired = n_mp % n_dp == 0 and n_mp % 2 == 0 and n_dp % 2 == 0
    return jax.shard_map(
        functools.partial(fused, n_dp, n_mp, STREAMS) if paired else local,
        mesh=mesh,
        in_specs=(
            P("dp", None, "mp"),
            P("dp", None, "mp"),
            P("mp", None),
            P(),
            P("dp", None, "mp"),
            P(),
            P(),
        ),
        out_specs=P("mp", "dp"),
        check_vma=False,
    )
```

```python
import functools

import jax
import jax.numpy as jnp
from jax import lax
from jax.experimental import pallas as pl
from jax.experimental.pallas import tpu as pltpu
from jax.sharding import PartitionSpec as P

MESH = pl.DeviceIdType.MESH
NT = (((1,), (1,)), ((), ()))
TN = (((0,), (0,)), ((), ()))
STREAMS = 2
F32 = jnp.float32
BF16 = jnp.bfloat16
MAXR = 3
BP = 2


EPS = 1e-06


def local(
    prelude_output, init_noise, core_weight, norm_gain, state_cotangent, step_counts, group_table
):
    full_width = core_weight.shape[1]
    local_width = core_weight.shape[0]
    slot_total = init_noise.shape[0]
    seq_length = init_noise.shape[1]
    row_count = slot_total * seq_length
    my_group = lax.axis_index("dp")
    column_first = lax.axis_index("mp") * local_width
    seq_total = group_table.shape[0]
    seq_index = jnp.arange(seq_total, dtype=jnp.int32)
    earlier = (group_table[:, None] == group_table[None, :]) & (
        seq_index[None, :] < seq_index[:, None]
    )
    slot_rank = jnp.sum(earlier.astype(jnp.int32), axis=1)
    selected_rows = (group_table[None, :] == my_group) & (
        slot_rank[None, :] == jnp.arange(slot_total, dtype=jnp.int32)[:, None]
    )
    slot_counts = jnp.sum(jnp.where(selected_rows, step_counts[None, :], 0), axis=1)
    chosen_weights = selected_rows.astype(jnp.bfloat16)
    injected_input = jnp.einsum(
        "br,ref->bef",
        chosen_weights,
        lax.all_gather(prelude_output, "dp", axis=0, tiled=True),
        preferred_element_type=jnp.float32,
    ).reshape(row_count, local_width)
    gain_local = lax.dynamic_slice_in_dim(norm_gain, column_first, local_width, 0)

    def feature_sum(values):
        return lax.psum(values, "mp")

    shard_state = init_noise.reshape(row_count, local_width)
    saved = []
    piece_rows = lax.all_gather(shard_state, "mp", axis=1, tiled=True)
    product = lax.dot_general(
        piece_rows, core_weight, (((1,), (1,)), ((), ())), preferred_element_type=jnp.float32
    )
    whole_state = piece_rows
    product, whole_state = (product, whole_state)
    for turn in range(MAXR):
        active = jnp.repeat(turn >= MAXR - slot_counts, seq_length)[:, None]
        if turn > 0:
            product = lax.dot_general(
                whole_state,
                core_weight,
                (((1,), (1,)), ((), ())),
                preferred_element_type=jnp.float32,
            )
        mixed = (product + injected_input).astype(jnp.bfloat16)
        mixed_float = mixed.astype(jnp.float32)
        if turn + 1 < MAXR:
            mixed_whole = lax.all_gather(mixed, "mp", axis=1, tiled=True).astype(jnp.float32)
            inverse_rms = lax.rsqrt(jnp.sum(mixed_whole * mixed_whole, axis=1) / full_width + EPS)
            renewed = (norm_gain * mixed_whole * inverse_rms[:, None]).astype(jnp.bfloat16)
            saved.append((whole_state, mixed_float, inverse_rms, active))
            whole_state = jnp.where(active, renewed, whole_state)
        else:
            inverse_rms = lax.rsqrt(
                feature_sum(jnp.sum(mixed_float * mixed_float, axis=1)) / full_width + EPS
            )
            saved.append((whole_state, mixed_float, inverse_rms, active))
    upstream = state_cotangent.reshape(row_count, local_width).astype(jnp.float32)
    weight_grad = jnp.zeros((local_width, full_width), jnp.float32)
    for back_index in range(BP):
        whole_state, mixed_float, inverse_rms, active = saved[MAXR - 1 - back_index]
        scaled = upstream * gain_local
        inner = feature_sum(jnp.sum(scaled * mixed_float, axis=1))
        delta = (
            inverse_rms[:, None] * scaled
            - mixed_float * (inverse_rms**3 * inner / full_width)[:, None]
        )
        delta_b = jnp.where(active, delta, 0.0).astype(jnp.bfloat16)
        weight_grad = weight_grad + lax.dot_general(
            delta_b, whole_state, (((0,), (0,)), ((), ())), preferred_element_type=jnp.float32
        )
        if back_index + 1 < BP:
            partial_rows = jnp.dot(delta_b, core_weight, preferred_element_type=jnp.float32)
            summed_rows = lax.psum_scatter(
                partial_rows.astype(jnp.bfloat16), "mp", scatter_dimension=1, tiled=True
            ).astype(jnp.float32)
            upstream = jnp.where(active, summed_rows, upstream)
    return lax.psum_scatter(
        weight_grad.astype(jnp.bfloat16), "dp", scatter_dimension=1, tiled=True
    ).astype(jnp.float32)


LANES = 128
GROUP = 16


def packed_rows(part_rows, width):
    rest = width % LANES
    if part_rows % GROUP or rest * (part_rows // GROUP) > LANES:
        return None
    return width // LANES * part_rows + (GROUP if rest else 0)


def pack(ref, values):
    part_rows, width = values.shape
    whole = width // LANES
    rest = width - whole * LANES
    for c in range(whole):
        ref[pl.ds(c * part_rows, part_rows)] = values[:, c * LANES : (c + 1) * LANES].astype(BF16)
    if rest:
        groups = part_rows // GROUP
        pieces = [
            values[g * GROUP : (g + 1) * GROUP, whole * LANES :].astype(F32) for g in range(groups)
        ]
        pieces.append(jnp.zeros((GROUP, LANES - groups * rest), F32))
        ref[pl.ds(whole * part_rows, GROUP)] = jnp.concatenate(pieces, axis=1).astype(BF16)


def unpack(ref, part_rows, width):
    whole = width // LANES
    rest = width - whole * LANES
    columns = [ref[pl.ds(c * part_rows, part_rows)].astype(F32) for c in range(whole)]
    if rest:
        last = ref[pl.ds(whole * part_rows, GROUP)].astype(F32)
        columns.append(
            jnp.concatenate(
                [last[:, g * rest : (g + 1) * rest] for g in range(part_rows // GROUP)], axis=0
            )
        )
    return jnp.concatenate(columns, axis=1)


def core_kernel(
    n_dp, n_mp, streams, full_width, cap,
    counts_in, groups_in, prelude_ref, noise_ref, cot_ref, gain_in, w_hbm,
    ds, xs,
    w_ref, w8, u0, u1, u2, y0, y1, gain_ref, counts_ref, pick_ref, inject, acc, square, scale, rms,
    cot_rows, scaled, y_last, delta_b, spread_own, total_ref, noise_rows,
    pre_all, noise_all, cot_all, red, pair_send, pair_recv, line_send, line_recv,
    w_sem, in_send, in_recv, g_send, g_recv, x_send, x_recv, own_sem, d_send, d_recv,
    red_send, red_recv, p_send, p_recv, l_send, l_recv,
):
    dp = lax.axis_index("dp")
    mp = lax.axis_index("mp")
    n_line = n_mp // 2
    line, side = mp // 2, lax.rem(mp, 2)
    blocks = n_mp // n_dp
    seq_dev, tokens, width = prelude_ref.shape
    rows = seq_dev * tokens
    part_rows = rows // streams

    w_copy = pltpu.make_async_copy(w_hbm, w_ref, w_sem)
    w_copy.start()

    barrier = pltpu.get_barrier_semaphore()
    for o in range(1, n_mp):
        pl.semaphore_signal(
            barrier, inc=1, device_id=(dp, lax.rem(mp + o, n_mp)), device_id_type=MESH
        )
    for o in range(1, n_dp):
        pl.semaphore_signal(
            barrier, inc=1, device_id=(lax.rem(dp + o, n_dp), mp), device_id_type=MESH
        )

    seqs = groups_in.shape[0]
    one, zero = jnp.int32(1), jnp.int32(0)
    group = [groups_in[i] for i in range(seqs)]
    rank = []
    for i in range(seqs):
        r = zero
        for j in range(i):
            r = r + jnp.where(group[j] == group[i], one, zero)
        rank.append(r)
    full = []
    for g in range(n_dp):
        size = zero
        for i in range(seqs):
            size = size + jnp.where(group[i] == g, one, zero)
        full.append(jnp.where(size == cap, one, zero))
    order = []
    for g in range(n_dp):
        r = zero
        for e in range(g):
            r = r + jnp.where(full[e] == full[g], one, zero)
        order.append(r)
    mine_full, mine_order = zero, zero
    for g in range(n_dp):
        mine_full = jnp.where(dp == g, full[g], mine_full)
        mine_order = jnp.where(dp == g, order[g], mine_order)
    partner = zero
    part_weight = []
    for g in range(n_dp):
        hit = full[g] * (one - mine_full) * jnp.where(order[g] == mine_order, one, zero)
        partner = partner + hit * g
        part_weight.append(hit.astype(F32))
    own_weight = mine_full.astype(F32)
    for b in range(seq_dev):
        want_group, want_rank = dp, jnp.int32(b)
        if b == seq_dev - 1:
            want_group = jnp.where(mine_full == one, dp, partner)
            want_rank = jnp.where(mine_full == one, want_rank, cap - 1)
        count = zero
        for i in range(seqs):
            hit = jnp.where(group[i] == want_group, one, zero) * jnp.where(
                rank[i] == want_rank, one, zero
            )
            count = count + hit * counts_in[i]
            pick_ref[b * seqs + i] = hit.astype(F32)
        counts_ref[pl.ds(b * tokens, tokens)] = jnp.zeros((tokens, 1), F32) + count.astype(F32)

    pl.semaphore_wait(barrier, n_mp + n_dp - 2)

    def remote(src, dst, send, recv, device):
        return pltpu.make_async_remote_copy(
            src_ref=src, dst_ref=dst, send_sem=send, recv_sem=recv,
            device_id=device, device_id_type=MESH,
        )

    in_copies = []

    def cross(which, src, dst):
        copies = []
        for o in range(1, n_dp):
            copy = remote(
                src, dst.at[dp], in_send.at[which, o], in_recv.at[which, o],
                (lax.rem(dp + o, n_dp), mp),
            )
            copy.start()
            copies.append(copy)
        in_copies.append(copies)

    cross(0, noise_ref.at[seq_dev], noise_all)
    peer = (dp, line * 2 + 1 - side)

    def gather_start(turn, s, buf):
        own = buf.at[s, mp]
        remote(own, own, g_send.at[turn, s, 1], g_recv.at[turn, s, 1], peer).start()
        for h in range(1, n_line):
            to = (dp, lax.rem(line + h, n_line) * 2 + side)
            remote(own, own, g_send.at[turn, s, 1 + h], g_recv.at[turn, s, 1 + h], to).start()

    def gather_wait(turn, s, buf, at, owner):
        remote(
            buf.at[s, owner], buf.at[s, owner], g_send.at[turn, s, at], g_recv.at[turn, s, at], peer
        ).wait_recv()

    def gather_forward(turn, s, buf, h):
        owner = lax.rem(line + n_line - h, n_line) * 2 + side
        gather_wait(turn, s, buf, 1 + h, owner)
        at = n_line + h
        remote(
            buf.at[s, owner], buf.at[s, owner], g_send.at[turn, s, at], g_recv.at[turn, s, at], peer
        ).start()

    def gather_steps(turn, s, buf, use, forwarded=False):
        def step(at, carry):
            h = jnp.where(at < 2, 0, jnp.where(at <= n_line, at - 1, at - n_line))
            other = jnp.where(at < 2, at, jnp.where(at <= n_line, 0, 1))
            owner = lax.rem(line + n_line - h, n_line) * 2 + lax.rem(side + other, 2)

            @pl.when((at == 1) | (at > n_line))
            def _():
                gather_wait(turn, s, buf, at, owner)

            if not forwarded:

                @pl.when((at >= 2) & (at <= n_line))
                def _():
                    gather_forward(turn, s, buf, h)

            use(owner)
            return carry

        lax.fori_loop(0, n_mp, step, 0)

    def each_stream(body):
        def step(s, carry):
            body(s)
            return carry

        lax.fori_loop(0, streams, step, 0)

    def third_rows(own, gathered):
        total = own_weight * own[seq_dev - 1].astype(F32)
        for q in range(n_dp):
            total = total + part_weight[q] * gathered[q].astype(F32)
        return total

    kept = (seq_dev - 1) * tokens
    for b in range(seq_dev - 1):
        noise_rows[pl.ds(b * tokens, tokens)] = noise_ref[b]

    def first_start(s):
        pack(u0.at[s, mp], noise_rows[pl.ds(s * part_rows, part_rows)])
        gather_start(0, s, u0)

    first_start(0)
    noise_all[dp] = noise_ref[seq_dev]
    for copy in in_copies[0]:
        copy.wait_recv()
    noise_rows[pl.ds(kept, tokens)] = third_rows(noise_ref, noise_all).astype(BF16)
    cross(1, prelude_ref, pre_all)
    cross(2, cot_ref.at[seq_dev], cot_all)
    pre_all[dp] = prelude_ref[...]
    cot_all[dp] = cot_ref[seq_dev]

    w_copy.wait()
    waiting = list(range(1, n_line))
    for k in range(n_mp):
        w8[k] = w_ref[:, k * width : (k + 1) * width]
        gain_ref[k] = gain_in[pl.ds(k * width, width)].reshape(1, width)
        if k >= 1 and waiting:
            gather_forward(0, 0, u0, waiting.pop(0))
            if not waiting:
                for s in range(1, streams):
                    first_start(s)

    for copy in in_copies[1]:
        copy.wait_recv()
    for b in range(seq_dev):

        def add(q, t, b=b):
            for i in range(seq_dev):
                t = t + pick_ref[b * seqs + q * seq_dev + i] * pre_all[q, i].astype(F32)
            return t

        inject[pl.ds(b * tokens, tokens)] = lax.fori_loop(
            0, n_dp, add, jnp.zeros((tokens, width), F32)
        )

    def rows_of(s):
        return pl.ds(pl.multiple_of(s * part_rows, part_rows), part_rows)

    def active(turn, s):
        return counts_ref[rows_of(s)] >= float(MAXR - turn)

    def first(s, forwarded):
        acc[s] = jnp.zeros((part_rows, width), F32)

        def use(k):
            acc[s] += lax.dot_general(
                unpack(u0.at[s, k], part_rows, width).astype(BF16), w8[k], NT, preferred_element_type=F32)

        gather_steps(0, s, u0, use, forwarded=forwarded)
        pack(y0.at[s, mp], acc[s] + inject[rows_of(s)])
        gather_start(1, s, y0)

    for s in range(streams):
        first(s, s == 0)

    def renew(turn, s, y_all, old_block, after):
        live = active(turn, s)
        acc[s] = jnp.zeros((part_rows, width), F32)
        square[...] = jnp.zeros_like(square)

        def use(k):
            y = unpack(y_all.at[s, k], part_rows, width)
            square[...] += jnp.sum(y * y, axis=1, keepdims=True)
            new = jnp.where(live, gain_ref[k] * y, old_block(k)).astype(BF16)
            after[s, k] = new
            acc[s] += lax.dot_general(new, w8[k], NT, preferred_element_type=F32)
            to = k // blocks
            part = lax.rem(k, blocks)
            dst = xs.at[part, turn, s, dp]

            @pl.when(to == dp)
            def _():
                pltpu.make_async_copy(after.at[s, k], dst, own_sem.at[turn, s, part]).start()

            @pl.when(to != dp)
            def _():
                remote(
                    after.at[s, k], dst, x_send.at[turn, s, k], x_recv.at[turn, s, dp, part],
                    (to, mp),
                ).start()

        gather_steps(1 + turn, s, y_all, use)
        root = lax.rsqrt(square[...] / full_width + EPS)
        rms[turn, rows_of(s)] = root
        previous = 1.0 if turn == 0 else scale[turn - 1, rows_of(s)]
        scale[turn, rows_of(s)] = jnp.where(live, root, previous)

    def second(s):
        renew(0, s, y0, lambda k: unpack(u0.at[s, k], part_rows, width), u1)
        pack(y1.at[s, mp], scale[0, rows_of(s)] * acc[s] + inject[rows_of(s)])
        gather_start(2, s, y1)

    each_stream(second)

    for copy in in_copies[2]:
        copy.wait_recv()
    gain = gain_ref[mp]
    cot_rows[pl.ds(kept, tokens)] = third_rows(cot_ref, cot_all)
    for b in range(seq_dev - 1):
        cot_rows[pl.ds(b * tokens, tokens)] = cot_ref[b].astype(F32)
    scaled[...] = cot_rows[...] * gain

    def sums_start(which, s, values):
        ones = jnp.ones((4, width), F32)
        lines = [
            lax.dot_general(
                ones, v, NT, preferred_element_type=F32, precision=lax.Precision.HIGHEST
            )
            for v in values
        ]
        red[which, s, mp] = jnp.concatenate(lines * (2 // len(lines)), axis=0)
        own = red.at[which, s, mp]
        for o in range(1, n_mp):
            remote(
                own, own, red_send.at[which, s, o], red_recv.at[which, s, o],
                (dp, lax.rem(mp + o, n_mp)),
            ).start()

    def sums_end(which, s):
        own = red.at[which, s, mp]
        for o in range(1, n_mp):
            remote(
                own, own, red_send.at[which, s, o], red_recv.at[which, s, o], peer
            ).wait_recv()
        total = red[which, s, 0]
        for k in range(1, n_mp):
            total = total + red[which, s, k]
        columns = jnp.transpose(total)
        return columns[:, 0:1], columns[:, 4:5]

    def third(s):
        renew(1, s, y1, lambda k: u1[s, k].astype(F32), u2)
        y = (scale[1, rows_of(s)] * acc[s] + inject[rows_of(s)]).astype(BF16).astype(F32)
        y_last[rows_of(s)] = y
        sums_start(0, s, (y * y, scaled[rows_of(s)] * y))

    each_stream(third)

    dp_pair, dp_side = dp // 2, lax.rem(dp, 2)
    n_pair = n_dp // 2
    dp_peer = (dp_pair * 2 + 1 - dp_side, mp)

    def spread_copies(which, s):
        own, dst = spread_own.at[which, s], ds.at[which, s, dp]
        copies = []
        for h in range(1, n_pair):
            to = (lax.rem(dp_pair + h, n_pair) * 2 + dp_side, mp)
            copies.append(remote(own, dst, d_send.at[which, s, h], d_recv.at[which, s, h], to))
        copies.append(remote(own, dst, d_send.at[which, s, 0], d_recv.at[which, s, 0], dp_peer))
        return copies, pltpu.make_async_copy(own, dst, own_sem.at[which, s, blocks])

    def spread_start(which, s, values):
        spread_own[which, s] = values
        copies, local_copy = spread_copies(which, s)
        for copy in copies:
            copy.start()
        local_copy.start()

    def spread_forwards(which, s):
        forwards = []
        for h in range(1, n_pair):
            held = ds.at[which, s, lax.rem(dp_pair + n_pair - h, n_pair) * 2 + dp_side]
            f = n_pair + h
            forwards.append(
                remote(held, held, d_send.at[which, s, f], d_recv.at[which, s, f], dp_peer)
            )
        return forwards

    def spread_forward(which, s):
        copies, unused = spread_copies(which, s)
        for copy, forward in zip(copies, spread_forwards(which, s)):
            copy.wait_recv()
            forward.start()

    def pair_copy(s, at):
        return remote(
            pair_send.at[s, at], pair_recv.at[s, at], p_send.at[s, at], p_recv.at[s, at], peer
        )

    def line_copy(s, at):
        to = (dp, lax.rem(line + at + 1, n_line) * 2 + side)
        return remote(
            line_send.at[s, at], line_recv.at[s, at], l_send.at[s, at], l_recv.at[s, at], to
        )

    def back_first(s):
        square2, inner2 = sums_end(0, s)
        root = lax.rsqrt(square2 / full_width + EPS)
        y = y_last[rows_of(s)]
        delta = jnp.where(
            active(2, s),
            root * scaled[rows_of(s)] - y * (root * root * root * inner2 / full_width),
            0.0,
        )
        delta_b[s] = delta.astype(BF16)

        def pair_step(at, carry):
            to_line = lax.rem(line + at + 1, n_line)
            product = jnp.dot(
                delta_b[s], w8[to_line * 2 + 1 - side], preferred_element_type=F32
            )
            pack(pair_send.at[s, at], product)
            pair_copy(s, at).start()
            return carry

        lax.fori_loop(0, n_line, pair_step, 0)
        spread_start(1, s, (delta * scale[1, rows_of(s)]).astype(BF16))
        inner = delta_b[s].astype(F32) * acc[s]
        sums_start(1, s, (inner,))

    each_stream(back_first)

    def back_second(s):
        def line_step(at, carry):
            to_line = lax.rem(line + at + 1, n_line)
            product = jnp.dot(delta_b[s], w8[to_line * 2 + side], preferred_element_type=F32)
            pair_copy(s, at).wait_recv()
            total = product.astype(BF16).astype(F32) + unpack(pair_recv.at[s, at], part_rows, width)
            total_ref[s] = total

            @pl.when(at < n_line - 1)
            def _():
                pack(line_send.at[s, at], total)
                line_copy(s, at).start()

            return carry

        lax.fori_loop(0, n_line, line_step, 0)

    each_stream(back_second)
    for s in range(streams):
        spread_forward(1, s)

    def back_third(s):
        unused, inner = sums_end(1, s)
        total = total_ref[s]
        for at in range(n_line - 1):
            line_copy(s, at).wait_recv()
            total = total + unpack(line_recv.at[s, at], part_rows, width)
        upstream = jnp.where(active(2, s), total, cot_rows[rows_of(s)])
        y = unpack(y1.at[s, mp], part_rows, width)
        root = rms[1, rows_of(s)]
        delta = jnp.where(
            active(1, s),
            root * (upstream * gain) - y * (root * root * root * inner / full_width),
            0.0,
        )
        spread_start(0, s, (delta * scale[0, rows_of(s)]).astype(BF16))

    each_stream(back_third)
    for s in range(streams):
        spread_forward(0, s)

    def finish(s):
        for which in range(BP):
            copies, local_copy = spread_copies(which, s)
            copies[-1].wait_recv()
            for copy in spread_forwards(which, s):
                copy.wait()
            for copy in copies:
                copy.wait_send()
            local_copy.wait()
            for part in range(blocks):
                pltpu.make_async_copy(
                    u1.at[s, 0], xs.at[part, which, s, dp], own_sem.at[which, s, part]
                ).wait()
                for h in range(1, n_dp):
                    q = lax.rem(dp + h, n_dp)
                    copy = remote(
                        u1.at[s, 0], xs.at[part, which, s, q],
                        x_send.at[which, s, q * blocks + part], x_recv.at[which, s, q, part],
                        (q, mp),
                    )
                    copy.wait()
            own = red.at[which, s, mp]
            for o in range(1, n_mp):
                remote(
                    own, own, red_send.at[which, s, o], red_recv.at[which, s, o], peer
                ).wait_send()
        for turn, buf in enumerate((u0, y0, y1)):
            for at in range(1, n_mp):
                remote(
                    buf.at[s, mp], buf.at[s, mp], g_send.at[turn, s, at], g_recv.at[turn, s, at],
                    peer,
                ).wait_send()
        for at in range(n_line):
            pair_copy(s, at).wait_send()
        for at in range(n_line - 1):
            line_copy(s, at).wait_send()

    each_stream(finish)
    for copies in in_copies:
        for copy in copies:
            copy.wait_send()


def grad_kernel(ds_ref, xs_ref, out_ref):
    width = ds_ref.shape[-1]
    left = ds_ref[...].reshape(-1, width)
    depth = left.shape[0]
    full = xs_ref.shape[-1]
    for part in range(xs_ref.shape[0]):
        right = xs_ref[part].reshape(depth, full)
        out_ref[:, part * full : (part + 1) * full] = lax.dot_general(
            left, right, TN, preferred_element_type=F32
        )


def fused(
    n_dp, n_mp, streams,
    prelude_output, init_noise, core_weight, norm_gain, state_cotangent, step_counts, group_table,
):
    width, full_width = core_weight.shape
    seq_dev, tokens = prelude_output.shape[:2]
    cap = init_noise.shape[0]
    seqs = group_table.shape[0]
    rows = seq_dev * tokens
    part_rows = rows // streams
    blocks = n_mp // n_dp
    n_line, n_pair = n_mp // 2, n_dp // 2
    vmem = pl.BlockSpec(memory_space=pltpu.VMEM)
    smem = pl.BlockSpec(memory_space=pltpu.SMEM)
    any_space = pl.BlockSpec(memory_space=pl.ANY)
    state = pltpu.VMEM((streams, n_mp, part_rows, width), BF16)
    row_f32 = pltpu.VMEM((rows, width), F32)
    stream_f32 = pltpu.VMEM((streams, part_rows, width), F32)
    packed = packed_rows(part_rows, width)
    travel = pltpu.VMEM((streams, n_mp, packed, LANES), BF16)
    pieces = pltpu.VMEM((streams, n_line, packed, LANES), BF16)
    dma = pltpu.SemaphoreType.DMA
    scratch = [
        pltpu.VMEM((width, full_width), BF16),
        pltpu.VMEM((n_mp, width, width), BF16),
        travel, state, state, travel, travel,
        pltpu.VMEM((n_mp, 1, width), F32),
        pltpu.VMEM((rows, 1), F32),
        pltpu.SMEM((seq_dev * seqs,), F32),
        row_f32, stream_f32,
        pltpu.VMEM((part_rows, 1), F32),
        pltpu.VMEM((BP, rows, 1), F32),
        pltpu.VMEM((BP, rows, 1), F32),
        row_f32, row_f32, row_f32,
        pltpu.VMEM((streams, part_rows, width), BF16),
        pltpu.VMEM((BP, streams, part_rows, width), BF16),
        stream_f32,
        pltpu.VMEM((rows, width), BF16),
        pltpu.VMEM((n_dp, seq_dev, tokens, width), BF16),
        pltpu.VMEM((n_dp, tokens, width), BF16),
        pltpu.VMEM((n_dp, tokens, width), BF16),
        pltpu.VMEM((BP, streams, n_mp, 8, part_rows), F32),
        pieces, pieces, pieces, pieces,
        dma,
        dma((3, n_dp)), dma((3, n_dp)),
        dma((MAXR, streams, n_mp)), dma((MAXR, streams, n_mp)),
        dma((BP, streams, n_mp)), dma((BP, streams, n_dp, blocks)),
        dma((BP, streams, blocks + 1)),
        dma((BP, streams, 2 * n_pair)), dma((BP, streams, 2 * n_pair)),
        dma((BP, streams, n_mp)), dma((BP, streams, n_mp)),
        dma((streams, n_line)), dma((streams, n_line)),
        dma((streams, n_line)), dma((streams, n_line)),
    ]
    deltas, states = pl.pallas_call(
        functools.partial(core_kernel, n_dp, n_mp, streams, full_width, cap),
        out_shape=(
            jax.ShapeDtypeStruct((BP, streams, n_dp, part_rows, width), BF16),
            jax.ShapeDtypeStruct((blocks, BP, streams, n_dp, part_rows, width), BF16),
        ),
        in_specs=[smem] * 2 + [vmem] * 4 + [any_space],
        out_specs=(any_space, any_space),
        scratch_shapes=scratch,
        compiler_params=pltpu.CompilerParams(
            collective_id=0, has_side_effects=True, vmem_limit_bytes=56 * 1024 * 1024
        ),
        cost_estimate=pl.CostEstimate(
            flops=2 * rows * full_width * width * 4, bytes_accessed=20_000_000, transcendentals=0
        ),
    )(
        step_counts, group_table, prelude_output, init_noise, state_cotangent,
        norm_gain, core_weight,
    )
    tile = 256
    return pl.pallas_call(
        grad_kernel,
        grid=(pl.cdiv(width, tile),),
        out_shape=jax.ShapeDtypeStruct((width, blocks * width), F32),
        in_specs=[
            pl.BlockSpec((BP, streams, n_dp, part_rows, tile), lambda i: (0, 0, 0, 0, i)),
            pl.BlockSpec(states.shape, lambda i: (0,) * 6),
        ],
        out_specs=pl.BlockSpec((tile, blocks * width), lambda i: (i, 0)),
        compiler_params=pltpu.CompilerParams(vmem_limit_bytes=60 * 1024 * 1024),
    )(deltas, states)


def solution(mesh):
    n_dp, n_mp = mesh.shape["dp"], mesh.shape["mp"]
    paired = n_mp % n_dp == 0 and n_mp % 2 == 0 and n_dp % 2 == 0
    return jax.shard_map(
        functools.partial(fused, n_dp, n_mp, STREAMS) if paired else local,
        mesh=mesh,
        in_specs=(
            P("dp", None, "mp"),
            P("dp", None, "mp"),
            P("mp", None),
            P(),
            P("dp", None, "mp"),
            P(),
            P(),
        ),
        out_specs=P("mp", "dp"),
        check_vma=False,
    )
```

```python
import functools

import jax
import jax.numpy as jnp
from jax import lax
from jax.experimental import pallas as pl
from jax.experimental.pallas import tpu as pltpu
from jax.sharding import PartitionSpec as P

MESH = pl.DeviceIdType.MESH
NT = (((1,), (1,)), ((), ()))
TN = (((0,), (0,)), ((), ()))
STREAMS = 2
F32 = jnp.float32
BF16 = jnp.bfloat16
MAXR = 3
BP = 2


EPS = 1e-06


def local(
    prelude_output, init_noise, core_weight, norm_gain, state_cotangent, step_counts, group_table
):
    full_width = core_weight.shape[1]
    local_width = core_weight.shape[0]
    slot_total = init_noise.shape[0]
    seq_length = init_noise.shape[1]
    row_count = slot_total * seq_length
    my_group = lax.axis_index("dp")
    column_first = lax.axis_index("mp") * local_width
    seq_total = group_table.shape[0]
    seq_index = jnp.arange(seq_total, dtype=jnp.int32)
    earlier = (group_table[:, None] == group_table[None, :]) & (
        seq_index[None, :] < seq_index[:, None]
    )
    slot_rank = jnp.sum(earlier.astype(jnp.int32), axis=1)
    selected_rows = (group_table[None, :] == my_group) & (
        slot_rank[None, :] == jnp.arange(slot_total, dtype=jnp.int32)[:, None]
    )
    slot_counts = jnp.sum(jnp.where(selected_rows, step_counts[None, :], 0), axis=1)
    chosen_weights = selected_rows.astype(jnp.bfloat16)
    injected_input = jnp.einsum(
        "br,ref->bef",
        chosen_weights,
        lax.all_gather(prelude_output, "dp", axis=0, tiled=True),
        preferred_element_type=jnp.float32,
    ).reshape(row_count, local_width)
    gain_local = lax.dynamic_slice_in_dim(norm_gain, column_first, local_width, 0)

    def feature_sum(values):
        return lax.psum(values, "mp")

    shard_state = init_noise.reshape(row_count, local_width)
    saved = []
    piece_rows = lax.all_gather(shard_state, "mp", axis=1, tiled=True)
    product = lax.dot_general(
        piece_rows, core_weight, (((1,), (1,)), ((), ())), preferred_element_type=jnp.float32
    )
    whole_state = piece_rows
    product, whole_state = (product, whole_state)
    for turn in range(MAXR):
        active = jnp.repeat(turn >= MAXR - slot_counts, seq_length)[:, None]
        if turn > 0:
            product = lax.dot_general(
                whole_state,
                core_weight,
                (((1,), (1,)), ((), ())),
                preferred_element_type=jnp.float32,
            )
        mixed = (product + injected_input).astype(jnp.bfloat16)
        mixed_float = mixed.astype(jnp.float32)
        if turn + 1 < MAXR:
            mixed_whole = lax.all_gather(mixed, "mp", axis=1, tiled=True).astype(jnp.float32)
            inverse_rms = lax.rsqrt(jnp.sum(mixed_whole * mixed_whole, axis=1) / full_width + EPS)
            renewed = (norm_gain * mixed_whole * inverse_rms[:, None]).astype(jnp.bfloat16)
            saved.append((whole_state, mixed_float, inverse_rms, active))
            whole_state = jnp.where(active, renewed, whole_state)
        else:
            inverse_rms = lax.rsqrt(
                feature_sum(jnp.sum(mixed_float * mixed_float, axis=1)) / full_width + EPS
            )
            saved.append((whole_state, mixed_float, inverse_rms, active))
    upstream = state_cotangent.reshape(row_count, local_width).astype(jnp.float32)
    weight_grad = jnp.zeros((local_width, full_width), jnp.float32)
    for back_index in range(BP):
        whole_state, mixed_float, inverse_rms, active = saved[MAXR - 1 - back_index]
        scaled = upstream * gain_local
        inner = feature_sum(jnp.sum(scaled * mixed_float, axis=1))
        delta = (
            inverse_rms[:, None] * scaled
            - mixed_float * (inverse_rms**3 * inner / full_width)[:, None]
        )
        delta_b = jnp.where(active, delta, 0.0).astype(jnp.bfloat16)
        weight_grad = weight_grad + lax.dot_general(
            delta_b, whole_state, (((0,), (0,)), ((), ())), preferred_element_type=jnp.float32
        )
        if back_index + 1 < BP:
            partial_rows = jnp.dot(delta_b, core_weight, preferred_element_type=jnp.float32)
            summed_rows = lax.psum_scatter(
                partial_rows.astype(jnp.bfloat16), "mp", scatter_dimension=1, tiled=True
            ).astype(jnp.float32)
            upstream = jnp.where(active, summed_rows, upstream)
    return lax.psum_scatter(
        weight_grad.astype(jnp.bfloat16), "dp", scatter_dimension=1, tiled=True
    ).astype(jnp.float32)


LANES = 128
GROUP = 16


def packed_rows(part_rows, width):
    rest = width % LANES
    if part_rows % GROUP or rest * (part_rows // GROUP) > LANES:
        return None
    return width // LANES * part_rows + (GROUP if rest else 0)


def pack(ref, values):
    part_rows, width = values.shape
    whole = width // LANES
    rest = width - whole * LANES
    for c in range(whole):
        ref[pl.ds(c * part_rows, part_rows)] = values[:, c * LANES : (c + 1) * LANES].astype(BF16)
    if rest:
        groups = part_rows // GROUP
        pieces = [
            values[g * GROUP : (g + 1) * GROUP, whole * LANES :].astype(F32) for g in range(groups)
        ]
        pieces.append(jnp.zeros((GROUP, LANES - groups * rest), F32))
        ref[pl.ds(whole * part_rows, GROUP)] = jnp.concatenate(pieces, axis=1).astype(BF16)


def unpack(ref, part_rows, width):
    whole = width // LANES
    rest = width - whole * LANES
    columns = [ref[pl.ds(c * part_rows, part_rows)].astype(F32) for c in range(whole)]
    if rest:
        last = ref[pl.ds(whole * part_rows, GROUP)].astype(F32)
        columns.append(
            jnp.concatenate(
                [last[:, g * rest : (g + 1) * rest] for g in range(part_rows // GROUP)], axis=0
            )
        )
    return jnp.concatenate(columns, axis=1)


def core_kernel(
    n_dp, n_mp, streams, full_width, cap,
    counts_in, groups_in, prelude_ref, noise_ref, cot_ref, gain_in, w_hbm,
    ds, xs,
    w_ref, w8, u0, u1, u2, y0, y1, gain_ref, counts_ref, pick_ref, inject, acc, square, scale, rms,
    cot_rows, scaled, y_last, delta_b, spread_own, total_ref, noise_rows,
    pre_all, noise_all, cot_all, red, pair_send, pair_recv, line_send, line_recv,
    w_sem, in_send, in_recv, g_send, g_recv, x_send, x_recv, own_sem, d_send, d_recv,
    red_send, red_recv, p_send, p_recv, l_send, l_recv,
):
    dp = lax.axis_index("dp")
    mp = lax.axis_index("mp")
    n_line = n_mp // 2
    line, side = mp // 2, lax.rem(mp, 2)
    blocks = n_mp // n_dp
    seq_dev, tokens, width = prelude_ref.shape
    rows = seq_dev * tokens
    part_rows = rows // streams

    w_copy = pltpu.make_async_copy(w_hbm, w_ref, w_sem)
    w_copy.start()

    barrier = pltpu.get_barrier_semaphore()
    for o in range(1, n_mp):
        pl.semaphore_signal(
            barrier, inc=1, device_id=(dp, lax.rem(mp + o, n_mp)), device_id_type=MESH
        )
    for o in range(1, n_dp):
        pl.semaphore_signal(
            barrier, inc=1, device_id=(lax.rem(dp + o, n_dp), mp), device_id_type=MESH
        )

    seqs = groups_in.shape[0]
    one, zero = jnp.int32(1), jnp.int32(0)
    group = [groups_in[i] for i in range(seqs)]
    rank = []
    for i in range(seqs):
        r = zero
        for j in range(i):
            r = r + jnp.where(group[j] == group[i], one, zero)
        rank.append(r)
    full = []
    for g in range(n_dp):
        size = zero
        for i in range(seqs):
            size = size + jnp.where(group[i] == g, one, zero)
        full.append(jnp.where(size == cap, one, zero))
    order = []
    for g in range(n_dp):
        r = zero
        for e in range(g):
            r = r + jnp.where(full[e] == full[g], one, zero)
        order.append(r)
    mine_full, mine_order = zero, zero
    for g in range(n_dp):
        mine_full = jnp.where(dp == g, full[g], mine_full)
        mine_order = jnp.where(dp == g, order[g], mine_order)
    partner = zero
    part_weight = []
    for g in range(n_dp):
        hit = full[g] * (one - mine_full) * jnp.where(order[g] == mine_order, one, zero)
        partner = partner + hit * g
        part_weight.append(hit.astype(F32))
    own_weight = mine_full.astype(F32)
    for b in range(seq_dev):
        want_group, want_rank = dp, jnp.int32(b)
        if b == seq_dev - 1:
            want_group = jnp.where(mine_full == one, dp, partner)
            want_rank = jnp.where(mine_full == one, want_rank, cap - 1)
        count = zero
        for i in range(seqs):
            hit = jnp.where(group[i] == want_group, one, zero) * jnp.where(
                rank[i] == want_rank, one, zero
            )
            count = count + hit * counts_in[i]
            pick_ref[b * seqs + i] = hit.astype(F32)
        counts_ref[pl.ds(b * tokens, tokens)] = jnp.zeros((tokens, 1), F32) + count.astype(F32)

    pl.semaphore_wait(barrier, n_mp + n_dp - 2)

    def remote(src, dst, send, recv, device):
        return pltpu.make_async_remote_copy(
            src_ref=src, dst_ref=dst, send_sem=send, recv_sem=recv,
            device_id=device, device_id_type=MESH,
        )

    in_copies = []

    def cross(which, src, dst):
        copies = []
        for o in range(1, n_dp):
            copy = remote(
                src, dst.at[dp], in_send.at[which, o], in_recv.at[which, o],
                (lax.rem(dp + o, n_dp), mp),
            )
            copy.start()
            copies.append(copy)
        in_copies.append(copies)

    cross(0, noise_ref.at[seq_dev], noise_all)
    peer = (dp, line * 2 + 1 - side)

    def gather_start(turn, s, buf):
        own = buf.at[s, mp]
        remote(own, own, g_send.at[turn, s, 1], g_recv.at[turn, s, 1], peer).start()
        for h in range(1, n_line):
            to = (dp, lax.rem(line + h, n_line) * 2 + side)
            remote(own, own, g_send.at[turn, s, 1 + h], g_recv.at[turn, s, 1 + h], to).start()

    def gather_wait(turn, s, buf, at, owner):
        remote(
            buf.at[s, owner], buf.at[s, owner], g_send.at[turn, s, at], g_recv.at[turn, s, at], peer
        ).wait_recv()

    def gather_forward(turn, s, buf, h):
        owner = lax.rem(line + n_line - h, n_line) * 2 + side
        gather_wait(turn, s, buf, 1 + h, owner)
        at = n_line + h
        remote(
            buf.at[s, owner], buf.at[s, owner], g_send.at[turn, s, at], g_recv.at[turn, s, at], peer
        ).start()

    def gather_steps(turn, s, buf, use, forwarded=False):
        if not forwarded:
            for h in range(1, n_line):
                gather_forward(turn, s, buf, h)

        def step(at, carry):
            h = jnp.where(at < 2, 0, jnp.where(at <= n_line, at - 1, at - n_line))
            other = jnp.where(at < 2, at, jnp.where(at <= n_line, 0, 1))
            owner = lax.rem(line + n_line - h, n_line) * 2 + lax.rem(side + other, 2)

            @pl.when((at == 1) | (at > n_line))
            def _():
                gather_wait(turn, s, buf, at, owner)

            use(owner)
            return carry

        lax.fori_loop(0, n_mp, step, 0)

    def each_stream(body):
        def step(s, carry):
            body(s)
            return carry

        lax.fori_loop(0, streams, step, 0)

    def third_rows(own, gathered):
        total = own_weight * own[seq_dev - 1].astype(F32)
        for q in range(n_dp):
            total = total + part_weight[q] * gathered[q].astype(F32)
        return total

    kept = (seq_dev - 1) * tokens
    for b in range(seq_dev - 1):
        noise_rows[pl.ds(b * tokens, tokens)] = noise_ref[b]

    def first_start(s):
        pack(u0.at[s, mp], noise_rows[pl.ds(s * part_rows, part_rows)])
        gather_start(0, s, u0)

    first_start(0)
    noise_all[dp] = noise_ref[seq_dev]
    for copy in in_copies[0]:
        copy.wait_recv()
    noise_rows[pl.ds(kept, tokens)] = third_rows(noise_ref, noise_all).astype(BF16)
    cross(1, prelude_ref, pre_all)
    cross(2, cot_ref.at[seq_dev], cot_all)
    pre_all[dp] = prelude_ref[...]
    cot_all[dp] = cot_ref[seq_dev]

    w_copy.wait()
    waiting = list(range(1, n_line))
    for k in range(n_mp):
        w8[k] = w_ref[:, k * width : (k + 1) * width]
        gain_ref[k] = gain_in[pl.ds(k * width, width)].reshape(1, width)
        if k >= 1 and waiting:
            gather_forward(0, 0, u0, waiting.pop(0))
            if not waiting:
                for s in range(1, streams):
                    first_start(s)

    for copy in in_copies[1]:
        copy.wait_recv()
    for b in range(seq_dev):

        def add(q, t, b=b):
            for i in range(seq_dev):
                t = t + pick_ref[b * seqs + q * seq_dev + i] * pre_all[q, i].astype(F32)
            return t

        inject[pl.ds(b * tokens, tokens)] = lax.fori_loop(
            0, n_dp, add, jnp.zeros((tokens, width), F32)
        )

    def rows_of(s):
        return pl.ds(pl.multiple_of(s * part_rows, part_rows), part_rows)

    def active(turn, s):
        return counts_ref[rows_of(s)] >= float(MAXR - turn)

    def first(s, forwarded):
        acc[s] = jnp.zeros((part_rows, width), F32)

        def use(k):
            acc[s] += lax.dot_general(
                unpack(u0.at[s, k], part_rows, width).astype(BF16), w8[k], NT, preferred_element_type=F32)

        gather_steps(0, s, u0, use, forwarded=forwarded)
        pack(y0.at[s, mp], acc[s] + inject[rows_of(s)])
        gather_start(1, s, y0)

    for s in range(streams):
        first(s, s == 0)

    def renew(turn, s, y_all, old_block, after):
        live = active(turn, s)
        acc[s] = jnp.zeros((part_rows, width), F32)
        square[...] = jnp.zeros_like(square)

        def use(k):
            y = unpack(y_all.at[s, k], part_rows, width)
            square[...] += jnp.sum(y * y, axis=1, keepdims=True)
            new = jnp.where(live, gain_ref[k] * y, old_block(k)).astype(BF16)
            after[s, k] = new
            acc[s] += lax.dot_general(new, w8[k], NT, preferred_element_type=F32)
            to = k // blocks
            part = lax.rem(k, blocks)
            dst = xs.at[part, turn, s, dp]

            @pl.when(to == dp)
            def _():
                pltpu.make_async_copy(after.at[s, k], dst, own_sem.at[turn, s, part]).start()

            @pl.when(to != dp)
            def _():
                remote(
                    after.at[s, k], dst, x_send.at[turn, s, k], x_recv.at[turn, s, dp, part],
                    (to, mp),
                ).start()

        gather_steps(1 + turn, s, y_all, use)
        root = lax.rsqrt(square[...] / full_width + EPS)
        rms[turn, rows_of(s)] = root
        previous = 1.0 if turn == 0 else scale[turn - 1, rows_of(s)]
        scale[turn, rows_of(s)] = jnp.where(live, root, previous)

    def second(s):
        renew(0, s, y0, lambda k: unpack(u0.at[s, k], part_rows, width), u1)
        pack(y1.at[s, mp], scale[0, rows_of(s)] * acc[s] + inject[rows_of(s)])
        gather_start(2, s, y1)

    each_stream(second)

    for copy in in_copies[2]:
        copy.wait_recv()
    gain = gain_ref[mp]
    cot_rows[pl.ds(kept, tokens)] = third_rows(cot_ref, cot_all)
    for b in range(seq_dev - 1):
        cot_rows[pl.ds(b * tokens, tokens)] = cot_ref[b].astype(F32)
    scaled[...] = cot_rows[...] * gain

    def sums_start(which, s, values):
        ones = jnp.ones((4, width), F32)
        lines = [
            lax.dot_general(
                ones, v, NT, preferred_element_type=F32, precision=lax.Precision.HIGHEST
            )
            for v in values
        ]
        red[which, s, mp] = jnp.concatenate(lines * (2 // len(lines)), axis=0)
        own = red.at[which, s, mp]
        for o in range(1, n_mp):
            remote(
                own, own, red_send.at[which, s, o], red_recv.at[which, s, o],
                (dp, lax.rem(mp + o, n_mp)),
            ).start()

    def sums_end(which, s):
        own = red.at[which, s, mp]
        for o in range(1, n_mp):
            remote(
                own, own, red_send.at[which, s, o], red_recv.at[which, s, o], peer
            ).wait_recv()
        total = red[which, s, 0]
        for k in range(1, n_mp):
            total = total + red[which, s, k]
        columns = jnp.transpose(total)
        return columns[:, 0:1], columns[:, 4:5]

    def third(s):
        renew(1, s, y1, lambda k: u1[s, k].astype(F32), u2)
        y = (scale[1, rows_of(s)] * acc[s] + inject[rows_of(s)]).astype(BF16).astype(F32)
        y_last[rows_of(s)] = y
        sums_start(0, s, (y * y, scaled[rows_of(s)] * y))

    each_stream(third)

    dp_pair, dp_side = dp // 2, lax.rem(dp, 2)
    n_pair = n_dp // 2
    dp_peer = (dp_pair * 2 + 1 - dp_side, mp)

    def spread_copies(which, s):
        own, dst = spread_own.at[which, s], ds.at[which, s, dp]
        copies = []
        for h in range(1, n_pair):
            to = (lax.rem(dp_pair + h, n_pair) * 2 + dp_side, mp)
            copies.append(remote(own, dst, d_send.at[which, s, h], d_recv.at[which, s, h], to))
        copies.append(remote(own, dst, d_send.at[which, s, 0], d_recv.at[which, s, 0], dp_peer))
        return copies, pltpu.make_async_copy(own, dst, own_sem.at[which, s, blocks])

    def spread_start(which, s, values):
        spread_own[which, s] = values
        copies, local_copy = spread_copies(which, s)
        for copy in copies:
            copy.start()
        local_copy.start()

    def spread_forwards(which, s):
        forwards = []
        for h in range(1, n_pair):
            held = ds.at[which, s, lax.rem(dp_pair + n_pair - h, n_pair) * 2 + dp_side]
            f = n_pair + h
            forwards.append(
                remote(held, held, d_send.at[which, s, f], d_recv.at[which, s, f], dp_peer)
            )
        return forwards

    def spread_forward(which, s):
        copies, unused = spread_copies(which, s)
        for copy, forward in zip(copies, spread_forwards(which, s)):
            copy.wait_recv()
            forward.start()

    def pair_copy(s, at):
        return remote(
            pair_send.at[s, at], pair_recv.at[s, at], p_send.at[s, at], p_recv.at[s, at], peer
        )

    def line_copy(s, at):
        to = (dp, lax.rem(line + at + 1, n_line) * 2 + side)
        return remote(
            line_send.at[s, at], line_recv.at[s, at], l_send.at[s, at], l_recv.at[s, at], to
        )

    def back_first(s):
        square2, inner2 = sums_end(0, s)
        root = lax.rsqrt(square2 / full_width + EPS)
        y = y_last[rows_of(s)]
        delta = jnp.where(
            active(2, s),
            root * scaled[rows_of(s)] - y * (root * root * root * inner2 / full_width),
            0.0,
        )
        delta_b[s] = delta.astype(BF16)

        def pair_step(at, carry):
            to_line = lax.rem(line + at + 1, n_line)
            product = jnp.dot(
                delta_b[s], w8[to_line * 2 + 1 - side], preferred_element_type=F32
            )
            pack(pair_send.at[s, at], product)
            pair_copy(s, at).start()
            return carry

        lax.fori_loop(0, n_line, pair_step, 0)
        spread_start(1, s, (delta * scale[1, rows_of(s)]).astype(BF16))
        inner = delta_b[s].astype(F32) * acc[s]
        sums_start(1, s, (inner,))

    each_stream(back_first)

    def back_second(s):
        def line_step(at, carry):
            to_line = lax.rem(line + at + 1, n_line)
            product = jnp.dot(delta_b[s], w8[to_line * 2 + side], preferred_element_type=F32)
            pair_copy(s, at).wait_recv()
            total = product.astype(BF16).astype(F32) + unpack(pair_recv.at[s, at], part_rows, width)
            total_ref[s] = total

            @pl.when(at < n_line - 1)
            def _():
                pack(line_send.at[s, at], total)
                line_copy(s, at).start()

            return carry

        lax.fori_loop(0, n_line, line_step, 0)

    each_stream(back_second)
    for s in range(streams):
        spread_forward(1, s)

    def back_third(s):
        unused, inner = sums_end(1, s)
        total = total_ref[s]
        for at in range(n_line - 1):
            line_copy(s, at).wait_recv()
            total = total + unpack(line_recv.at[s, at], part_rows, width)
        upstream = jnp.where(active(2, s), total, cot_rows[rows_of(s)])
        y = unpack(y1.at[s, mp], part_rows, width)
        root = rms[1, rows_of(s)]
        delta = jnp.where(
            active(1, s),
            root * (upstream * gain) - y * (root * root * root * inner / full_width),
            0.0,
        )
        spread_start(0, s, (delta * scale[0, rows_of(s)]).astype(BF16))

    each_stream(back_third)
    for s in range(streams):
        spread_forward(0, s)

    def finish(s):
        for which in range(BP):
            copies, local_copy = spread_copies(which, s)
            copies[-1].wait_recv()
            for copy in spread_forwards(which, s):
                copy.wait()
            for copy in copies:
                copy.wait_send()
            local_copy.wait()
            for part in range(blocks):
                pltpu.make_async_copy(
                    u1.at[s, 0], xs.at[part, which, s, dp], own_sem.at[which, s, part]
                ).wait()
                for h in range(1, n_dp):
                    q = lax.rem(dp + h, n_dp)
                    copy = remote(
                        u1.at[s, 0], xs.at[part, which, s, q],
                        x_send.at[which, s, q * blocks + part], x_recv.at[which, s, q, part],
                        (q, mp),
                    )
                    copy.wait()
            own = red.at[which, s, mp]
            for o in range(1, n_mp):
                remote(
                    own, own, red_send.at[which, s, o], red_recv.at[which, s, o], peer
                ).wait_send()
        for turn, buf in enumerate((u0, y0, y1)):
            for at in range(1, n_mp):
                remote(
                    buf.at[s, mp], buf.at[s, mp], g_send.at[turn, s, at], g_recv.at[turn, s, at],
                    peer,
                ).wait_send()
        for at in range(n_line):
            pair_copy(s, at).wait_send()
        for at in range(n_line - 1):
            line_copy(s, at).wait_send()

    each_stream(finish)
    for copies in in_copies:
        for copy in copies:
            copy.wait_send()


def grad_kernel(ds_ref, xs_ref, out_ref):
    width = ds_ref.shape[-1]
    left = ds_ref[...].reshape(-1, width)
    depth = left.shape[0]
    full = xs_ref.shape[-1]
    for part in range(xs_ref.shape[0]):
        right = xs_ref[part].reshape(depth, full)
        out_ref[:, part * full : (part + 1) * full] = lax.dot_general(
            left, right, TN, preferred_element_type=F32
        )


def fused(
    n_dp, n_mp, streams,
    prelude_output, init_noise, core_weight, norm_gain, state_cotangent, step_counts, group_table,
):
    width, full_width = core_weight.shape
    seq_dev, tokens = prelude_output.shape[:2]
    cap = init_noise.shape[0]
    seqs = group_table.shape[0]
    rows = seq_dev * tokens
    part_rows = rows // streams
    blocks = n_mp // n_dp
    n_line, n_pair = n_mp // 2, n_dp // 2
    vmem = pl.BlockSpec(memory_space=pltpu.VMEM)
    smem = pl.BlockSpec(memory_space=pltpu.SMEM)
    any_space = pl.BlockSpec(memory_space=pl.ANY)
    state = pltpu.VMEM((streams, n_mp, part_rows, width), BF16)
    row_f32 = pltpu.VMEM((rows, width), F32)
    stream_f32 = pltpu.VMEM((streams, part_rows, width), F32)
    packed = packed_rows(part_rows, width)
    travel = pltpu.VMEM((streams, n_mp, packed, LANES), BF16)
    pieces = pltpu.VMEM((streams, n_line, packed, LANES), BF16)
    dma = pltpu.SemaphoreType.DMA
    scratch = [
        pltpu.VMEM((width, full_width), BF16),
        pltpu.VMEM((n_mp, width, width), BF16),
        travel, state, state, travel, travel,
        pltpu.VMEM((n_mp, 1, width), F32),
        pltpu.VMEM((rows, 1), F32),
        pltpu.SMEM((seq_dev * seqs,), F32),
        row_f32, stream_f32,
        pltpu.VMEM((part_rows, 1), F32),
        pltpu.VMEM((BP, rows, 1), F32),
        pltpu.VMEM((BP, rows, 1), F32),
        row_f32, row_f32, row_f32,
        pltpu.VMEM((streams, part_rows, width), BF16),
        pltpu.VMEM((BP, streams, part_rows, width), BF16),
        stream_f32,
        pltpu.VMEM((rows, width), BF16),
        pltpu.VMEM((n_dp, seq_dev, tokens, width), BF16),
        pltpu.VMEM((n_dp, tokens, width), BF16),
        pltpu.VMEM((n_dp, tokens, width), BF16),
        pltpu.VMEM((BP, streams, n_mp, 8, part_rows), F32),
        pieces, pieces, pieces, pieces,
        dma,
        dma((3, n_dp)), dma((3, n_dp)),
        dma((MAXR, streams, n_mp)), dma((MAXR, streams, n_mp)),
        dma((BP, streams, n_mp)), dma((BP, streams, n_dp, blocks)),
        dma((BP, streams, blocks + 1)),
        dma((BP, streams, 2 * n_pair)), dma((BP, streams, 2 * n_pair)),
        dma((BP, streams, n_mp)), dma((BP, streams, n_mp)),
        dma((streams, n_line)), dma((streams, n_line)),
        dma((streams, n_line)), dma((streams, n_line)),
    ]
    deltas, states = pl.pallas_call(
        functools.partial(core_kernel, n_dp, n_mp, streams, full_width, cap),
        out_shape=(
            jax.ShapeDtypeStruct((BP, streams, n_dp, part_rows, width), BF16),
            jax.ShapeDtypeStruct((blocks, BP, streams, n_dp, part_rows, width), BF16),
        ),
        in_specs=[smem] * 2 + [vmem] * 4 + [any_space],
        out_specs=(any_space, any_space),
        scratch_shapes=scratch,
        compiler_params=pltpu.CompilerParams(
            collective_id=0, has_side_effects=True, vmem_limit_bytes=56 * 1024 * 1024
        ),
        cost_estimate=pl.CostEstimate(
            flops=2 * rows * full_width * width * 4, bytes_accessed=20_000_000, transcendentals=0
        ),
    )(
        step_counts, group_table, prelude_output, init_noise, state_cotangent,
        norm_gain, core_weight,
    )
    tile = 256
    return pl.pallas_call(
        grad_kernel,
        grid=(pl.cdiv(width, tile),),
        out_shape=jax.ShapeDtypeStruct((width, blocks * width), F32),
        in_specs=[
            pl.BlockSpec((BP, streams, n_dp, part_rows, tile), lambda i: (0, 0, 0, 0, i)),
            pl.BlockSpec(states.shape, lambda i: (0,) * 6),
        ],
        out_specs=pl.BlockSpec((tile, blocks * width), lambda i: (i, 0)),
        compiler_params=pltpu.CompilerParams(vmem_limit_bytes=60 * 1024 * 1024),
    )(deltas, states)


def solution(mesh):
    n_dp, n_mp = mesh.shape["dp"], mesh.shape["mp"]
    paired = n_mp % n_dp == 0 and n_mp % 2 == 0 and n_dp % 2 == 0
    return jax.shard_map(
        functools.partial(fused, n_dp, n_mp, STREAMS) if paired else local,
        mesh=mesh,
        in_specs=(
            P("dp", None, "mp"),
            P("dp", None, "mp"),
            P("mp", None),
            P(),
            P("dp", None, "mp"),
            P(),
            P(),
        ),
        out_specs=P("mp", "dp"),
        check_vma=False,
    )
```

```python
import functools

import jax
import jax.numpy as jnp
from jax import lax
from jax.experimental import pallas as pl
from jax.experimental.pallas import tpu as pltpu
from jax.sharding import PartitionSpec as P

MESH = pl.DeviceIdType.MESH
NT = (((1,), (1,)), ((), ()))
TN = (((0,), (0,)), ((), ()))
STREAMS = 2
F32 = jnp.float32
BF16 = jnp.bfloat16
MAXR = 3
BP = 2


EPS = 1e-06


def local(
    prelude_output, init_noise, core_weight, norm_gain, state_cotangent, step_counts, group_table
):
    full_width = core_weight.shape[1]
    local_width = core_weight.shape[0]
    slot_total = init_noise.shape[0]
    seq_length = init_noise.shape[1]
    row_count = slot_total * seq_length
    my_group = lax.axis_index("dp")
    column_first = lax.axis_index("mp") * local_width
    seq_total = group_table.shape[0]
    seq_index = jnp.arange(seq_total, dtype=jnp.int32)
    earlier = (group_table[:, None] == group_table[None, :]) & (
        seq_index[None, :] < seq_index[:, None]
    )
    slot_rank = jnp.sum(earlier.astype(jnp.int32), axis=1)
    selected_rows = (group_table[None, :] == my_group) & (
        slot_rank[None, :] == jnp.arange(slot_total, dtype=jnp.int32)[:, None]
    )
    slot_counts = jnp.sum(jnp.where(selected_rows, step_counts[None, :], 0), axis=1)
    chosen_weights = selected_rows.astype(jnp.bfloat16)
    injected_input = jnp.einsum(
        "br,ref->bef",
        chosen_weights,
        lax.all_gather(prelude_output, "dp", axis=0, tiled=True),
        preferred_element_type=jnp.float32,
    ).reshape(row_count, local_width)
    gain_local = lax.dynamic_slice_in_dim(norm_gain, column_first, local_width, 0)

    def feature_sum(values):
        return lax.psum(values, "mp")

    shard_state = init_noise.reshape(row_count, local_width)
    saved = []
    piece_rows = lax.all_gather(shard_state, "mp", axis=1, tiled=True)
    product = lax.dot_general(
        piece_rows, core_weight, (((1,), (1,)), ((), ())), preferred_element_type=jnp.float32
    )
    whole_state = piece_rows
    product, whole_state = (product, whole_state)
    for turn in range(MAXR):
        active = jnp.repeat(turn >= MAXR - slot_counts, seq_length)[:, None]
        if turn > 0:
            product = lax.dot_general(
                whole_state,
                core_weight,
                (((1,), (1,)), ((), ())),
                preferred_element_type=jnp.float32,
            )
        mixed = (product + injected_input).astype(jnp.bfloat16)
        mixed_float = mixed.astype(jnp.float32)
        if turn + 1 < MAXR:
            mixed_whole = lax.all_gather(mixed, "mp", axis=1, tiled=True).astype(jnp.float32)
            inverse_rms = lax.rsqrt(jnp.sum(mixed_whole * mixed_whole, axis=1) / full_width + EPS)
            renewed = (norm_gain * mixed_whole * inverse_rms[:, None]).astype(jnp.bfloat16)
            saved.append((whole_state, mixed_float, inverse_rms, active))
            whole_state = jnp.where(active, renewed, whole_state)
        else:
            inverse_rms = lax.rsqrt(
                feature_sum(jnp.sum(mixed_float * mixed_float, axis=1)) / full_width + EPS
            )
            saved.append((whole_state, mixed_float, inverse_rms, active))
    upstream = state_cotangent.reshape(row_count, local_width).astype(jnp.float32)
    weight_grad = jnp.zeros((local_width, full_width), jnp.float32)
    for back_index in range(BP):
        whole_state, mixed_float, inverse_rms, active = saved[MAXR - 1 - back_index]
        scaled = upstream * gain_local
        inner = feature_sum(jnp.sum(scaled * mixed_float, axis=1))
        delta = (
            inverse_rms[:, None] * scaled
            - mixed_float * (inverse_rms**3 * inner / full_width)[:, None]
        )
        delta_b = jnp.where(active, delta, 0.0).astype(jnp.bfloat16)
        weight_grad = weight_grad + lax.dot_general(
            delta_b, whole_state, (((0,), (0,)), ((), ())), preferred_element_type=jnp.float32
        )
        if back_index + 1 < BP:
            partial_rows = jnp.dot(delta_b, core_weight, preferred_element_type=jnp.float32)
            summed_rows = lax.psum_scatter(
                partial_rows.astype(jnp.bfloat16), "mp", scatter_dimension=1, tiled=True
            ).astype(jnp.float32)
            upstream = jnp.where(active, summed_rows, upstream)
    return lax.psum_scatter(
        weight_grad.astype(jnp.bfloat16), "dp", scatter_dimension=1, tiled=True
    ).astype(jnp.float32)


LANES = 128
GROUP = 16


def packed_rows(part_rows, width):
    rest = width % LANES
    if part_rows % GROUP or rest * (part_rows // GROUP) > LANES:
        return None
    return width // LANES * part_rows + (GROUP if rest else 0)


def pack(ref, values):
    part_rows, width = values.shape
    whole = width // LANES
    rest = width - whole * LANES
    for c in range(whole):
        ref[pl.ds(c * part_rows, part_rows)] = values[:, c * LANES : (c + 1) * LANES].astype(BF16)
    if rest:
        groups = part_rows // GROUP
        pieces = [
            values[g * GROUP : (g + 1) * GROUP, whole * LANES :].astype(F32) for g in range(groups)
        ]
        pieces.append(jnp.zeros((GROUP, LANES - groups * rest), F32))
        ref[pl.ds(whole * part_rows, GROUP)] = jnp.concatenate(pieces, axis=1).astype(BF16)


def unpack(ref, part_rows, width):
    whole = width // LANES
    rest = width - whole * LANES
    columns = [ref[pl.ds(c * part_rows, part_rows)].astype(F32) for c in range(whole)]
    if rest:
        last = ref[pl.ds(whole * part_rows, GROUP)].astype(F32)
        columns.append(
            jnp.concatenate(
                [last[:, g * rest : (g + 1) * rest] for g in range(part_rows // GROUP)], axis=0
            )
        )
    return jnp.concatenate(columns, axis=1)


def core_kernel(
    n_dp, n_mp, streams, full_width, cap,
    counts_in, groups_in, prelude_ref, noise_ref, cot_ref, gain_in, w_hbm,
    ds, xs,
    w_ref, w8, u0, u1, u2, y0, y1, gain_ref, counts_ref, pick_ref, inject, acc, square, scale, rms,
    cot_rows, scaled, y_last, delta_b, spread_own, total_ref, noise_rows,
    pre_all, noise_all, cot_all, red, pair_send, pair_recv, line_send, line_recv,
    w_sem, in_send, in_recv, g_send, g_recv, x_send, x_recv, own_sem, d_send, d_recv,
    red_send, red_recv, p_send, p_recv, l_send, l_recv,
):
    dp = lax.axis_index("dp")
    mp = lax.axis_index("mp")
    n_line = n_mp // 2
    line, side = mp // 2, lax.rem(mp, 2)
    blocks = n_mp // n_dp
    seq_dev, tokens, width = prelude_ref.shape
    rows = seq_dev * tokens
    part_rows = rows // streams

    w_copy = pltpu.make_async_copy(w_hbm, w_ref, w_sem)
    w_copy.start()

    barrier = pltpu.get_barrier_semaphore()
    for o in range(1, n_mp):
        pl.semaphore_signal(
            barrier, inc=1, device_id=(dp, lax.rem(mp + o, n_mp)), device_id_type=MESH
        )
    for o in range(1, n_dp):
        pl.semaphore_signal(
            barrier, inc=1, device_id=(lax.rem(dp + o, n_dp), mp), device_id_type=MESH
        )

    seqs = groups_in.shape[0]
    one, zero = jnp.int32(1), jnp.int32(0)
    group = [groups_in[i] for i in range(seqs)]
    rank = []
    for i in range(seqs):
        r = zero
        for j in range(i):
            r = r + jnp.where(group[j] == group[i], one, zero)
        rank.append(r)
    full = []
    for g in range(n_dp):
        size = zero
        for i in range(seqs):
            size = size + jnp.where(group[i] == g, one, zero)
        full.append(jnp.where(size == cap, one, zero))
    order = []
    for g in range(n_dp):
        r = zero
        for e in range(g):
            r = r + jnp.where(full[e] == full[g], one, zero)
        order.append(r)
    mine_full, mine_order = zero, zero
    for g in range(n_dp):
        mine_full = jnp.where(dp == g, full[g], mine_full)
        mine_order = jnp.where(dp == g, order[g], mine_order)
    partner = zero
    part_weight = []
    for g in range(n_dp):
        hit = full[g] * (one - mine_full) * jnp.where(order[g] == mine_order, one, zero)
        partner = partner + hit * g
        part_weight.append(hit.astype(F32))
    own_weight = mine_full.astype(F32)
    for b in range(seq_dev):
        want_group, want_rank = dp, jnp.int32(b)
        if b == seq_dev - 1:
            want_group = jnp.where(mine_full == one, dp, partner)
            want_rank = jnp.where(mine_full == one, want_rank, cap - 1)
        count = zero
        for i in range(seqs):
            hit = jnp.where(group[i] == want_group, one, zero) * jnp.where(
                rank[i] == want_rank, one, zero
            )
            count = count + hit * counts_in[i]
            pick_ref[b * seqs + i] = hit.astype(F32)
        counts_ref[pl.ds(b * tokens, tokens)] = jnp.zeros((tokens, 1), F32) + count.astype(F32)

    pl.semaphore_wait(barrier, n_mp + n_dp - 2)

    def remote(src, dst, send, recv, device):
        return pltpu.make_async_remote_copy(
            src_ref=src, dst_ref=dst, send_sem=send, recv_sem=recv,
            device_id=device, device_id_type=MESH,
        )

    in_copies = []

    def cross(which, src, dst):
        copies = []
        for o in range(1, n_dp):
            copy = remote(
                src, dst.at[dp], in_send.at[which, o], in_recv.at[which, o],
                (lax.rem(dp + o, n_dp), mp),
            )
            copy.start()
            copies.append(copy)
        in_copies.append(copies)

    cross(0, noise_ref.at[seq_dev], noise_all)
    peer = (dp, line * 2 + 1 - side)

    def gather_start(turn, s, buf):
        own = buf.at[s, mp]
        remote(own, own, g_send.at[turn, s, 1], g_recv.at[turn, s, 1], peer).start()
        for h in range(1, n_line):
            to = (dp, lax.rem(line + h, n_line) * 2 + side)
            remote(own, own, g_send.at[turn, s, 1 + h], g_recv.at[turn, s, 1 + h], to).start()

    def gather_wait(turn, s, buf, at, owner):
        remote(
            buf.at[s, owner], buf.at[s, owner], g_send.at[turn, s, at], g_recv.at[turn, s, at], peer
        ).wait_recv()

    def gather_forward(turn, s, buf, h):
        owner = lax.rem(line + n_line - h, n_line) * 2 + side
        gather_wait(turn, s, buf, 1 + h, owner)
        at = n_line + h
        remote(
            buf.at[s, owner], buf.at[s, owner], g_send.at[turn, s, at], g_recv.at[turn, s, at], peer
        ).start()

    def gather_forwards(turn, s, buf):
        for h in range(1, n_line):
            gather_forward(turn, s, buf, h)

    def gather_steps(turn, s, buf, use, forwarded=False):
        if not forwarded:
            gather_forwards(turn, s, buf)

        def step(at, carry):
            h = jnp.where(at < 2, 0, jnp.where(at <= n_line, at - 1, at - n_line))
            other = jnp.where(at < 2, at, jnp.where(at <= n_line, 0, 1))
            owner = lax.rem(line + n_line - h, n_line) * 2 + lax.rem(side + other, 2)

            @pl.when((at == 1) | (at > n_line))
            def _():
                gather_wait(turn, s, buf, at, owner)

            use(owner)
            return carry

        lax.fori_loop(0, n_mp, step, 0)

    def each_stream(body):
        def step(s, carry):
            body(s)
            return carry

        lax.fori_loop(0, streams, step, 0)

    def third_rows(own, gathered):
        total = own_weight * own[seq_dev - 1].astype(F32)
        for q in range(n_dp):
            total = total + part_weight[q] * gathered[q].astype(F32)
        return total

    kept = (seq_dev - 1) * tokens
    for b in range(seq_dev - 1):
        noise_rows[pl.ds(b * tokens, tokens)] = noise_ref[b]

    def first_start(s):
        pack(u0.at[s, mp], noise_rows[pl.ds(s * part_rows, part_rows)])
        gather_start(0, s, u0)

    first_start(0)
    noise_all[dp] = noise_ref[seq_dev]
    for copy in in_copies[0]:
        copy.wait_recv()
    noise_rows[pl.ds(kept, tokens)] = third_rows(noise_ref, noise_all).astype(BF16)
    cross(1, prelude_ref, pre_all)
    cross(2, cot_ref.at[seq_dev], cot_all)
    pre_all[dp] = prelude_ref[...]
    cot_all[dp] = cot_ref[seq_dev]

    w_copy.wait()
    waiting = list(range(1, n_line))
    for k in range(n_mp):
        w8[k] = w_ref[:, k * width : (k + 1) * width]
        gain_ref[k] = gain_in[pl.ds(k * width, width)].reshape(1, width)
        if k >= 1 and waiting:
            gather_forward(0, 0, u0, waiting.pop(0))
            if not waiting:
                for s in range(1, streams):
                    first_start(s)

    for copy in in_copies[1]:
        copy.wait_recv()
    for b in range(seq_dev):

        def add(q, t, b=b):
            for i in range(seq_dev):
                t = t + pick_ref[b * seqs + q * seq_dev + i] * pre_all[q, i].astype(F32)
            return t

        inject[pl.ds(b * tokens, tokens)] = lax.fori_loop(
            0, n_dp, add, jnp.zeros((tokens, width), F32)
        )

    def rows_of(s):
        return pl.ds(pl.multiple_of(s * part_rows, part_rows), part_rows)

    def active(turn, s):
        return counts_ref[rows_of(s)] >= float(MAXR - turn)

    def first(s, forwarded):
        acc[s] = jnp.zeros((part_rows, width), F32)

        def use(k):
            acc[s] += lax.dot_general(
                unpack(u0.at[s, k], part_rows, width).astype(BF16), w8[k], NT, preferred_element_type=F32)

        gather_steps(0, s, u0, use, forwarded=forwarded)
        pack(y0.at[s, mp], acc[s] + inject[rows_of(s)])
        gather_start(1, s, y0)

    for s in range(streams):
        first(s, s == 0)

    def renew(turn, s, y_all, old_block, after, forwarded=False):
        live = active(turn, s)
        acc[s] = jnp.zeros((part_rows, width), F32)
        square[...] = jnp.zeros_like(square)

        def use(k):
            y = unpack(y_all.at[s, k], part_rows, width)
            square[...] += jnp.sum(y * y, axis=1, keepdims=True)
            new = jnp.where(live, gain_ref[k] * y, old_block(k)).astype(BF16)
            after[s, k] = new
            acc[s] += lax.dot_general(new, w8[k], NT, preferred_element_type=F32)
            to = k // blocks
            part = lax.rem(k, blocks)
            dst = xs.at[part, turn, s, dp]

            @pl.when(to == dp)
            def _():
                pltpu.make_async_copy(after.at[s, k], dst, own_sem.at[turn, s, part]).start()

            @pl.when(to != dp)
            def _():
                remote(
                    after.at[s, k], dst, x_send.at[turn, s, k], x_recv.at[turn, s, dp, part],
                    (to, mp),
                ).start()

        gather_steps(1 + turn, s, y_all, use, forwarded=forwarded)
        root = lax.rsqrt(square[...] / full_width + EPS)
        rms[turn, rows_of(s)] = root
        previous = 1.0 if turn == 0 else scale[turn - 1, rows_of(s)]
        scale[turn, rows_of(s)] = jnp.where(live, root, previous)

    def second(s):
        renew(0, s, y0, lambda k: unpack(u0.at[s, k], part_rows, width), u1)
        pack(y1.at[s, mp], scale[0, rows_of(s)] * acc[s] + inject[rows_of(s)])
        gather_start(2, s, y1)

    each_stream(second)

    for copy in in_copies[2]:
        copy.wait_recv()
    gain = gain_ref[mp]
    cot_rows[pl.ds(kept, tokens)] = third_rows(cot_ref, cot_all)
    for b in range(seq_dev - 1):
        cot_rows[pl.ds(b * tokens, tokens)] = cot_ref[b].astype(F32)
    scaled[...] = cot_rows[...] * gain

    def sums_start(which, s, values):
        ones = jnp.ones((4, width), F32)
        lines = [
            lax.dot_general(
                ones, v, NT, preferred_element_type=F32, precision=lax.Precision.HIGHEST
            )
            for v in values
        ]
        red[which, s, mp] = jnp.concatenate(lines * (2 // len(lines)), axis=0)
        own = red.at[which, s, mp]
        for o in range(1, n_mp):
            remote(
                own, own, red_send.at[which, s, o], red_recv.at[which, s, o],
                (dp, lax.rem(mp + o, n_mp)),
            ).start()

    def sums_end(which, s):
        own = red.at[which, s, mp]
        for o in range(1, n_mp):
            remote(
                own, own, red_send.at[which, s, o], red_recv.at[which, s, o], peer
            ).wait_recv()
        total = red[which, s, 0]
        for k in range(1, n_mp):
            total = total + red[which, s, k]
        columns = jnp.transpose(total)
        return columns[:, 0:1], columns[:, 4:5]

    def third(s, forwarded):
        renew(1, s, y1, lambda k: u1[s, k].astype(F32), u2, forwarded=forwarded)
        y = (scale[1, rows_of(s)] * acc[s] + inject[rows_of(s)]).astype(BF16).astype(F32)
        y_last[rows_of(s)] = y
        sums_start(0, s, (y * y, scaled[rows_of(s)] * y))

    dp_pair, dp_side = dp // 2, lax.rem(dp, 2)
    n_pair = n_dp // 2
    dp_peer = (dp_pair * 2 + 1 - dp_side, mp)

    def spread_copies(which, s):
        own, dst = spread_own.at[which, s], ds.at[which, s, dp]
        copies = []
        for h in range(1, n_pair):
            to = (lax.rem(dp_pair + h, n_pair) * 2 + dp_side, mp)
            copies.append(remote(own, dst, d_send.at[which, s, h], d_recv.at[which, s, h], to))
        copies.append(remote(own, dst, d_send.at[which, s, 0], d_recv.at[which, s, 0], dp_peer))
        return copies, pltpu.make_async_copy(own, dst, own_sem.at[which, s, blocks])

    def spread_start(which, s, values):
        spread_own[which, s] = values
        copies, local_copy = spread_copies(which, s)
        for copy in copies:
            copy.start()
        local_copy.start()

    def spread_forwards(which, s):
        forwards = []
        for h in range(1, n_pair):
            held = ds.at[which, s, lax.rem(dp_pair + n_pair - h, n_pair) * 2 + dp_side]
            f = n_pair + h
            forwards.append(
                remote(held, held, d_send.at[which, s, f], d_recv.at[which, s, f], dp_peer)
            )
        return forwards

    def spread_forward(which, s):
        copies, unused = spread_copies(which, s)
        for copy, forward in zip(copies, spread_forwards(which, s)):
            copy.wait_recv()
            forward.start()

    def pair_copy(s, at):
        return remote(
            pair_send.at[s, at], pair_recv.at[s, at], p_send.at[s, at], p_recv.at[s, at], peer
        )

    def line_copy(s, at):
        to = (dp, lax.rem(line + at + 1, n_line) * 2 + side)
        return remote(
            line_send.at[s, at], line_recv.at[s, at], l_send.at[s, at], l_recv.at[s, at], to
        )

    def back_first(s):
        square2, inner2 = sums_end(0, s)
        root = lax.rsqrt(square2 / full_width + EPS)
        y = y_last[rows_of(s)]
        delta = jnp.where(
            active(2, s),
            root * scaled[rows_of(s)] - y * (root * root * root * inner2 / full_width),
            0.0,
        )
        delta_b[s] = delta.astype(BF16)

        def pair_step(at, carry):
            to_line = lax.rem(line + at + 1, n_line)
            product = jnp.dot(
                delta_b[s], w8[to_line * 2 + 1 - side], preferred_element_type=F32
            )
            pack(pair_send.at[s, at], product)
            pair_copy(s, at).start()
            return carry

        lax.fori_loop(0, n_line, pair_step, 0)
        spread_start(1, s, (delta * scale[1, rows_of(s)]).astype(BF16))
        inner = delta_b[s].astype(F32) * acc[s]
        sums_start(1, s, (inner,))

    def back_second(s):
        def line_step(at, carry):
            to_line = lax.rem(line + at + 1, n_line)
            product = jnp.dot(delta_b[s], w8[to_line * 2 + side], preferred_element_type=F32)
            pair_copy(s, at).wait_recv()
            total = product.astype(BF16).astype(F32) + unpack(pair_recv.at[s, at], part_rows, width)
            total_ref[s] = total

            @pl.when(at < n_line - 1)
            def _():
                pack(line_send.at[s, at], total)
                line_copy(s, at).start()

            return carry

        lax.fori_loop(0, n_line, line_step, 0)

    third(0, False)
    for s in range(1, streams):
        gather_forwards(2, s, y1)
        back_first(s - 1)
        third(s, True)
        back_second(s - 1)
    back_first(streams - 1)
    back_second(streams - 1)
    for s in range(streams):
        spread_forward(1, s)

    def back_third(s):
        unused, inner = sums_end(1, s)
        total = total_ref[s]
        for at in range(n_line - 1):
            line_copy(s, at).wait_recv()
            total = total + unpack(line_recv.at[s, at], part_rows, width)
        upstream = jnp.where(active(2, s), total, cot_rows[rows_of(s)])
        y = unpack(y1.at[s, mp], part_rows, width)
        root = rms[1, rows_of(s)]
        delta = jnp.where(
            active(1, s),
            root * (upstream * gain) - y * (root * root * root * inner / full_width),
            0.0,
        )
        spread_start(0, s, (delta * scale[0, rows_of(s)]).astype(BF16))

    each_stream(back_third)
    for s in range(streams):
        spread_forward(0, s)

    def finish(s):
        for which in range(BP):
            copies, local_copy = spread_copies(which, s)
            copies[-1].wait_recv()
            for copy in spread_forwards(which, s):
                copy.wait()
            for copy in copies:
                copy.wait_send()
            local_copy.wait()
            for part in range(blocks):
                pltpu.make_async_copy(
                    u1.at[s, 0], xs.at[part, which, s, dp], own_sem.at[which, s, part]
                ).wait()
                for h in range(1, n_dp):
                    q = lax.rem(dp + h, n_dp)
                    copy = remote(
                        u1.at[s, 0], xs.at[part, which, s, q],
                        x_send.at[which, s, q * blocks + part], x_recv.at[which, s, q, part],
                        (q, mp),
                    )
                    copy.wait()
            own = red.at[which, s, mp]
            for o in range(1, n_mp):
                remote(
                    own, own, red_send.at[which, s, o], red_recv.at[which, s, o], peer
                ).wait_send()
        for turn, buf in enumerate((u0, y0, y1)):
            for at in range(1, n_mp):
                remote(
                    buf.at[s, mp], buf.at[s, mp], g_send.at[turn, s, at], g_recv.at[turn, s, at],
                    peer,
                ).wait_send()
        for at in range(n_line):
            pair_copy(s, at).wait_send()
        for at in range(n_line - 1):
            line_copy(s, at).wait_send()

    each_stream(finish)
    for copies in in_copies:
        for copy in copies:
            copy.wait_send()


def grad_kernel(ds_ref, xs_ref, out_ref):
    width = ds_ref.shape[-1]
    left = ds_ref[...].reshape(-1, width)
    depth = left.shape[0]
    full = xs_ref.shape[-1]
    for part in range(xs_ref.shape[0]):
        right = xs_ref[part].reshape(depth, full)
        out_ref[:, part * full : (part + 1) * full] = lax.dot_general(
            left, right, TN, preferred_element_type=F32
        )


def fused(
    n_dp, n_mp, streams,
    prelude_output, init_noise, core_weight, norm_gain, state_cotangent, step_counts, group_table,
):
    width, full_width = core_weight.shape
    seq_dev, tokens = prelude_output.shape[:2]
    cap = init_noise.shape[0]
    seqs = group_table.shape[0]
    rows = seq_dev * tokens
    part_rows = rows // streams
    blocks = n_mp // n_dp
    n_line, n_pair = n_mp // 2, n_dp // 2
    vmem = pl.BlockSpec(memory_space=pltpu.VMEM)
    smem = pl.BlockSpec(memory_space=pltpu.SMEM)
    any_space = pl.BlockSpec(memory_space=pl.ANY)
    state = pltpu.VMEM((streams, n_mp, part_rows, width), BF16)
    row_f32 = pltpu.VMEM((rows, width), F32)
    stream_f32 = pltpu.VMEM((streams, part_rows, width), F32)
    packed = packed_rows(part_rows, width)
    travel = pltpu.VMEM((streams, n_mp, packed, LANES), BF16)
    pieces = pltpu.VMEM((streams, n_line, packed, LANES), BF16)
    dma = pltpu.SemaphoreType.DMA
    scratch = [
        pltpu.VMEM((width, full_width), BF16),
        pltpu.VMEM((n_mp, width, width), BF16),
        travel, state, state, travel, travel,
        pltpu.VMEM((n_mp, 1, width), F32),
        pltpu.VMEM((rows, 1), F32),
        pltpu.SMEM((seq_dev * seqs,), F32),
        row_f32, stream_f32,
        pltpu.VMEM((part_rows, 1), F32),
        pltpu.VMEM((BP, rows, 1), F32),
        pltpu.VMEM((BP, rows, 1), F32),
        row_f32, row_f32, row_f32,
        pltpu.VMEM((streams, part_rows, width), BF16),
        pltpu.VMEM((BP, streams, part_rows, width), BF16),
        stream_f32,
        pltpu.VMEM((rows, width), BF16),
        pltpu.VMEM((n_dp, seq_dev, tokens, width), BF16),
        pltpu.VMEM((n_dp, tokens, width), BF16),
        pltpu.VMEM((n_dp, tokens, width), BF16),
        pltpu.VMEM((BP, streams, n_mp, 8, part_rows), F32),
        pieces, pieces, pieces, pieces,
        dma,
        dma((3, n_dp)), dma((3, n_dp)),
        dma((MAXR, streams, n_mp)), dma((MAXR, streams, n_mp)),
        dma((BP, streams, n_mp)), dma((BP, streams, n_dp, blocks)),
        dma((BP, streams, blocks + 1)),
        dma((BP, streams, 2 * n_pair)), dma((BP, streams, 2 * n_pair)),
        dma((BP, streams, n_mp)), dma((BP, streams, n_mp)),
        dma((streams, n_line)), dma((streams, n_line)),
        dma((streams, n_line)), dma((streams, n_line)),
    ]
    deltas, states = pl.pallas_call(
        functools.partial(core_kernel, n_dp, n_mp, streams, full_width, cap),
        out_shape=(
            jax.ShapeDtypeStruct((BP, streams, n_dp, part_rows, width), BF16),
            jax.ShapeDtypeStruct((blocks, BP, streams, n_dp, part_rows, width), BF16),
        ),
        in_specs=[smem] * 2 + [vmem] * 4 + [any_space],
        out_specs=(any_space, any_space),
        scratch_shapes=scratch,
        compiler_params=pltpu.CompilerParams(
            collective_id=0, has_side_effects=True, vmem_limit_bytes=56 * 1024 * 1024
        ),
        cost_estimate=pl.CostEstimate(
            flops=2 * rows * full_width * width * 4, bytes_accessed=20_000_000, transcendentals=0
        ),
    )(
        step_counts, group_table, prelude_output, init_noise, state_cotangent,
        norm_gain, core_weight,
    )
    tile = 256
    return pl.pallas_call(
        grad_kernel,
        grid=(pl.cdiv(width, tile),),
        out_shape=jax.ShapeDtypeStruct((width, blocks * width), F32),
        in_specs=[
            pl.BlockSpec((BP, streams, n_dp, part_rows, tile), lambda i: (0, 0, 0, 0, i)),
            pl.BlockSpec(states.shape, lambda i: (0,) * 6),
        ],
        out_specs=pl.BlockSpec((tile, blocks * width), lambda i: (i, 0)),
        compiler_params=pltpu.CompilerParams(vmem_limit_bytes=60 * 1024 * 1024),
    )(deltas, states)


def solution(mesh):
    n_dp, n_mp = mesh.shape["dp"], mesh.shape["mp"]
    paired = n_mp % n_dp == 0 and n_mp % 2 == 0 and n_dp % 2 == 0
    return jax.shard_map(
        functools.partial(fused, n_dp, n_mp, STREAMS) if paired else local,
        mesh=mesh,
        in_specs=(
            P("dp", None, "mp"),
            P("dp", None, "mp"),
            P("mp", None),
            P(),
            P("dp", None, "mp"),
            P(),
            P(),
        ),
        out_specs=P("mp", "dp"),
        check_vma=False,
    )
```
